256 devices in a mesh: region: 32 (over z, y), sub: 8 (over x, core).
Axes of the slice: x: 4, y: 4, z: 8, core: 2. Of those that a mesh axis runs over, the one named last changes fastest.
Arguments:
- rhs: float32 [4096, 8, 768], P(('region', 'sub')), may hold values from -6 to 6
- diag_inv: bfloat16 [4096, 8, 8, 768], P(('region', 'sub'))
- coupling: bfloat16 [4096, 4, 8, 8, 768], P(('region', 'sub')), may hold values from -0.59765625 to 0.59765625
- neighbours: int32 [4096, 4], P(('region', 'sub')), may hold values from 0 to 47
- send_tiles: int32 [256, 8], P(('region', 'sub')), may hold values from 0 to 15, as said below
- tile_count: int32 [256], P(('region', 'sub')), may hold values from 1 to 16
- hessian: bfloat16 [4096, 6, 6, 768], P(('region', 'sub')), may hold values from -6 to 6
- shared_vertex: int32 [262144], P(('region', 'sub')), may hold values from 0 to 12287
- owner_region: int32 [262144, 1], P(('region', 'sub')), may hold values from 0 to 31; in each aligned block of 1024 rows (0 to 1023, 1024 to 2047, ...) at most 128 rows name the same one
- owner_slot: int32 [262144], P(('region', 'sub')), may hold values from 0 to 1023
Outputs:
- adjoint: float32 [4096, 8, 768], P(('region', 'sub'))
- metric: float32 [4096, 6, 768], P(('region', 'sub'))
- owned_metric: float32 [6, 262144], P(None, ('region', 'sub'))
The draws below stay inside these ranges and needn't reach their ends.
Inputs may be any that keep to these rules, and one draw needn't show every extreme that they name: `send_tiles`: within one device the 8 entries are distinct. `owner_region`: among the 1024 entries of one device no partition is named more than 128 times.
All inputs are finite; a program needn't handle non-finite values.
Results may differ from the reference program's by a relative error of at most 0.00055.
Values sent between devices are 32-bit elements; how exact they have to be, the bound alone decides.
No kernel may reach another device: no remote copies, remote signals or barrier semaphores. Data moves between devices by JAX's collectives and lax.ppermute only.
A program may use at most 128 MiB of HBM per device.

```python
import math
import jax
import jax.numpy as jnp
import numpy as np
from jax import lax

V = 768
BLOCK = 8
NVAR = 6
NEIGH = 4
SWEEPS = 3
CAP = 128
TD = 16
HS = 8
EXT = 48
SHARED = 1024
OWNED = 1024
RANKS = 256
TILES = 4096
SHARED_ALL = 262144
OWNED_ALL = 262144
N_REGION = 32
N_SUB = 8


def draw_diag_inv(key, part):
    key = jax.random.fold_in(key, 5)
    k_diag, k_off = jax.random.split(key)
    scale = jnp.exp(jax.random.uniform(k_diag, (TILES, 1, BLOCK, V), jnp.float32, jnp.log(0.4), jnp.log(1.0)))
    off = 0.08 * jax.random.normal(k_off, (TILES, BLOCK, BLOCK, V), jnp.float32)
    eye = jnp.eye(BLOCK, dtype=jnp.float32)[None, :, :, None]
    return (eye * scale + off).astype(jnp.bfloat16)


def draw_send_tiles(key, part):
    key = jax.random.fold_in(key, 11)
    keys = jax.random.split(key, RANKS)
    orders = jax.vmap(lambda k: jax.random.permutation(k, TD))(keys)
    return orders[:, :HS].astype(jnp.int32)


def draw_tile_count(key, part):
    key = jax.random.fold_in(key, 23)
    k_base, k_top, k_low = jax.random.split(key, 3)
    counts = jax.random.randint(k_base, (RANKS,), 1, TD + 1)
    top = jax.random.randint(k_top, (), 0, RANKS)
    low = (top + 1 + jax.random.randint(k_low, (), 0, RANKS - 1)) % RANKS
    counts = counts.at[top].set(TD).at[low].set(1)
    return counts.astype(jnp.int32)


def plant(entries, rng, smallest, top_value):
    index_at = [jax.random.randint(jax.random.fold_in(rng, axis), (), 0, length) for axis, length in enumerate(entries.shape)]
    longest = entries.shape.index(max(entries.shape))
    neighbour = index_at[:longest] + [(index_at[longest] + 1) % entries.shape[longest]] + index_at[longest + 1:]
    return entries.at[tuple(index_at)].set(smallest).at[tuple(neighbour)].set(top_value)


def steps_of(stream_key, extent, shards, least, high):
    factor_of = 1.0
    for position, shards_of in shards:
        draws = jax.random.uniform(jax.random.fold_in(jax.random.fold_in(stream_key, 6), position), (shards_of,), jnp.float32, least / len(shards), high / len(shards))
        factor_of = factor_of * jnp.repeat(jnp.exp(draws), extent[position] // shards_of).reshape((-1,) + (1,) * (len(extent) - 1 - position))
    return factor_of


def deal_out(rng, own, number, rows, count, top, reach, skew):
    sequence = jax.random.permutation(rng, count)
    heavy_load, common = shares(count, rows * top, reach, skew, True), shares(count, rows * top, reach, skew, False)
    places = jnp.arange(count)

    def named(sizes, turn):
        used = int((sizes > 0).sum())
        fixed = max(1, used // 4)
        passed = fixed + (places - fixed + turn * (used - fixed)) % max(1, count - fixed)
        return jnp.zeros((count,), jnp.int32).at[sequence[jnp.where(places < fixed, places, passed)]].set(jnp.asarray(sizes, jnp.int32))

    sizes = jnp.where(number % 4 == 0, named(heavy_load, number // 4), named(common, number - number // 4 - 1))
    mixed = jax.random.permutation(jax.random.fold_in(own, 3), count)
    giver, sink = mixed[0:count // 2 * 2:2], mixed[1:count // 2 * 2:2]
    margin = jnp.minimum(sizes[giver] - 1, reach - sizes[sink]) // 2
    margin = jnp.where((giver == sequence[0]) | (sink == sequence[0]) | (sizes[sink] == 0), 0, jnp.maximum(margin, 0))
    passed = jax.random.randint(jax.random.fold_in(own, 4), (count // 2,), 0, 1 << 20) % (margin + 1)
    sizes = sizes.at[giver].add(-passed).at[sink].add(passed)
    items = jnp.searchsorted(jnp.cumsum(sizes), jnp.arange(rows * top), side="right").astype(jnp.int32)
    table = items.reshape(top, rows).T
    table = table[jax.random.permutation(jax.random.fold_in(own, 1), rows)]
    turn = jax.random.randint(jax.random.fold_in(own, 2), (rows, 1), 0, top)
    return jnp.take_along_axis(table, (jnp.arange(top)[None, :] + turn) % top, axis=1)


def shares(count, total, limit, slope, full):
    loads = [(1 << 20) // math.isqrt(rank ** slope) + 1 for rank in range(1, count + 1)]
    largest = limit if full else min(limit, max(-(-total // count), total * loads[0] // sum(loads)))
    least = 1 if total - largest >= count - 1 else 0
    given, rest = [largest] + [least] * (count - 1), total - largest - least * (count - 1)
    while rest > 0:
        candidates = [i for i in range(1, count) if given[i] < largest] or [i for i in range(1, count) if given[i] < limit]
        whole, budget = sum([loads[i] for i in candidates]), rest
        for i in candidates:
            addition = min(limit - given[i], max(1, budget * loads[i] // whole), rest)
            given[i] = given[i] + addition
            rest = rest - addition
    return np.array(given)


def bell_draw(own_key, dims, deviation, reach, cuts=(), held_as=jnp.bfloat16):
    loudness = steps_of(own_key, dims, cuts, -0.22, 0.18) if cuts else 1.0
    values = jax.random.normal(own_key, dims, jnp.float32) * deviation * loudness
    return jnp.minimum(jnp.maximum(values, -reach), reach).astype(held_as)


def setup_inputs(seed: int = 0) -> dict:
    key_list = jax.random.split(jax.random.key(seed), 11)
    rhs = bell_draw(key_list[0], (TILES, BLOCK, V), 1.0, 6.0, ((0, 256),), jnp.float32)
    diag_inv = draw_diag_inv(jax.random.fold_in(key_list[10], 71), 0)
    coupling = bell_draw(key_list[2], (TILES, NEIGH, BLOCK, BLOCK, V), 0.1, 0.59765625, ((0, 256),))
    neighbours = plant(jax.random.randint(key_list[3], (TILES, NEIGH), 0, EXT), jax.random.fold_in(key_list[3], 1), 0, EXT - 1).astype(jnp.int32)
    send_tiles = draw_send_tiles(jax.random.fold_in(key_list[10], 71), 0)
    tile_count = draw_tile_count(jax.random.fold_in(key_list[10], 71), 0)
    hessian = bell_draw(key_list[6], (TILES, NVAR, 6, V), 1.0, 6.0, ((0, 256),))
    shared_vertex = plant(jax.random.randint(key_list[7], (SHARED_ALL,), 0, TD * V), jax.random.fold_in(key_list[7], 1), 0, (TD * V) - 1).astype(jnp.int32)
    owner_region_keys = jax.random.split(jax.random.fold_in(key_list[8], 1), SHARED_ALL // SHARED)
    owner_region_turns = jax.random.permutation(jax.random.fold_in(key_list[8], 3), SHARED_ALL // SHARED)
    owner_region = jax.vmap(lambda own, number: deal_out(jax.random.fold_in(key_list[8], 2), own, number, SHARED, N_REGION, 1, CAP, 2))(owner_region_keys, owner_region_turns).reshape((SHARED_ALL, 1))
    owner_slot = plant(jax.random.randint(key_list[9], (SHARED_ALL,), 0, OWNED), jax.random.fold_in(key_list[9], 1), 0, OWNED - 1).astype(jnp.int32)
    return {"rhs": rhs, "diag_inv": diag_inv, "coupling": coupling, "neighbours": neighbours, "send_tiles": send_tiles, "tile_count": tile_count, "hessian": hessian, "shared_vertex": shared_vertex, "owner_region": owner_region, "owner_slot": owner_slot}


def solve_blocks(inv, resid, live):
    out = jnp.einsum('tjiv,tjv->tiv', inv.astype(jnp.float32), resid)
    rows = (jnp.arange(BLOCK) < NVAR).astype(jnp.float32)
    return out * live[:, None, None] * rows[None, :, None]


def reference(rhs, diag_inv, coupling, neighbours, send_tiles, tile_count, hessian, shared_vertex, owner_region, owner_slot):
    live_all = (jnp.arange(TD)[None, :] < tile_count[:, None]).astype(jnp.float32)
    rhs_r = rhs.reshape(RANKS, TD, BLOCK, V)
    inv_r = diag_inv.reshape(RANKS, TD, BLOCK, BLOCK, V)
    cpl_r = coupling.reshape(RANKS, TD, NEIGH, BLOCK, BLOCK, V)
    nbr_r = neighbours.reshape(RANKS, TD, NEIGH)
    adjoint = lax.map(lambda a: solve_blocks(a[0], a[1], a[2]), (inv_r, rhs_r, live_all))
    send_g = send_tiles.reshape(N_REGION, N_SUB, HS)
    for sweep in range(SWEEPS):
        grid = adjoint.reshape(N_REGION, N_SUB, TD, BLOCK, V)
        sent = jnp.take_along_axis(grid, send_g[:, :, :, None, None], axis=2)
        zero_r = jnp.zeros((1, N_SUB, HS, BLOCK, V), jnp.float32)
        zero_s = jnp.zeros((N_REGION, 1, HS, BLOCK, V), jnp.float32)
        from_rlow = jnp.concatenate([zero_r, sent[:-1]], axis=0)
        from_rhigh = jnp.concatenate([sent[1:], zero_r], axis=0)
        from_slow = jnp.concatenate([zero_s, sent[:, :-1]], axis=1)
        from_shigh = jnp.concatenate([sent[:, 1:], zero_s], axis=1)
        extended = jnp.concatenate([grid, from_rlow, from_rhigh, from_slow, from_shigh], axis=2)
        extended = extended.reshape(RANKS, EXT, BLOCK, V)

        def update(item):
            ext_one, rhs_one, inv_one, cpl_one, nbr_one, live_one = item
            near = ext_one[nbr_one]
            pull = jnp.einsum('tkmjv,tkmv->tjv', cpl_one.astype(jnp.float32), near)
            return solve_blocks(inv_one, rhs_one - pull, live_one)

        adjoint = lax.map(update, (extended, rhs_r, inv_r, cpl_r, nbr_r, live_all))
    adjoint = adjoint.reshape(TILES, BLOCK, V)
    metric = jnp.einsum('tcv,tcsv->tsv', jnp.abs(adjoint[:, :NVAR]), hessian.astype(jnp.float32))
    flat = metric.reshape(RANKS, TD, 6, V).transpose(0, 2, 1, 3).reshape(RANKS, 6, TD * V)
    local = shared_vertex.reshape(RANKS, SHARED)
    values = jnp.take_along_axis(flat, local[:, None, :], axis=2)
    values = values.transpose(0, 2, 1).reshape(SHARED_ALL, 6)
    sub_of = (jnp.arange(SHARED_ALL, dtype=jnp.int32) // SHARED) % N_SUB
    target = (owner_region[:, 0] * N_SUB + sub_of) * OWNED + owner_slot
    owned = jax.ops.segment_sum(values, target.astype(jnp.int32), num_segments=OWNED_ALL)
    return adjoint, metric, owned.T
```

```python
import functools

import jax
import jax.numpy as jnp
from jax import lax
from jax.experimental import pallas as pl
from jax.experimental.pallas import tpu as pltpu
from jax.sharding import PartitionSpec as P

NVAR = 6
SWEEPS = 3
OWNED = 1024
CAP = 128
LANES = 128

F32 = jnp.float32
BF16 = jnp.bfloat16

VMEM = pl.BlockSpec(memory_space=pltpu.VMEM)
SMEM = pl.BlockSpec(memory_space=pltpu.SMEM)


def solve_tile(t, resid, inv_ref, live):
    total = None
    for j in range(inv_ref.shape[1]):
        term = inv_ref[t, j].astype(F32) * resid[pl.ds(j, 1), :]
        total = term if total is None else total + term
    rows = lax.broadcasted_iota(jnp.int32, total.shape, 0)
    return jnp.where((rows < NVAR) & live, total, 0.0)


def pack_sent(adj_ref, send_ref, sent_ref):
    for s in range(send_ref.shape[1]):
        tile = adj_ref[pl.ds(pl.multiple_of(send_ref[0, s] * 8, 8), 8), :]
        sent_ref[NVAR * s : NVAR * (s + 1), :] = tile[:NVAR]


def first_kernel(send_ref, count_ref, rhs_ref, inv_ref, adj_ref, sent_ref):
    tiles = rhs_ref.shape[0]

    @pl.loop(0, tiles)
    def _(t):
        out = solve_tile(t, rhs_ref.at[t], inv_ref, t < count_ref[0])
        adj_ref[pl.ds(pl.multiple_of(t * 8, 8), 8), :] = out

    pack_sent(adj_ref, send_ref, sent_ref)


def build_extended(old_ref, halo_refs, ext_ref):
    own = old_ref.shape[0]
    ext_ref[:own, :] = old_ref[...]
    odd_region = lax.axis_index("region") % 2
    odd_sub = lax.axis_index("sub") % 2
    places = (1 - odd_region, odd_region, 3 - odd_sub, 2 + odd_sub)
    width = halo_refs[0].shape[0]
    for place, halo in zip(places, halo_refs):
        ext_ref[pl.ds(pl.multiple_of(own + place * width, 8), width), :] = halo[...]


def pull_and_solve(t, near_ref, count_ref, rhs_ref, inv_ref, cpl_ref, ext_ref, resid_ref):
    own = rhs_ref.shape[0]
    acc = rhs_ref[t]
    for k in range(cpl_ref.shape[1]):
        tile = near_ref[t, k]
        base = jnp.where(tile < own, tile * 8, tile * NVAR + own * (8 - NVAR))
        for m in range(NVAR):
            acc = acc - cpl_ref[t, k, m].astype(F32) * ext_ref[pl.ds(base + m, 1), :]
    resid_ref[...] = acc
    return solve_tile(t, resid_ref, inv_ref, t < count_ref[0])


def sweep_kernel(
    near_ref, send_ref, count_ref, rhs_ref, inv_ref, cpl_ref, old_ref, h0, h1, h2, h3,
    adj_ref, sent_ref, ext_ref, resid_ref,
):
    build_extended(old_ref, (h0, h1, h2, h3), ext_ref)

    @pl.loop(0, rhs_ref.shape[0])
    def _(t):
        out = pull_and_solve(t, near_ref, count_ref, rhs_ref, inv_ref, cpl_ref, ext_ref, resid_ref)
        adj_ref[pl.ds(pl.multiple_of(t * 8, 8), 8), :] = out

    pack_sent(adj_ref, send_ref, sent_ref)


def last_kernel(
    near_ref, count_ref, rhs_ref, inv_ref, cpl_ref, hess_ref, old_ref, h0, h1, h2, h3,
    vertex_ref, region_ref, slot_ref, rank_hot_ref,
    adj_ref, metric_ref, parcel_ref, ext_ref, resid_ref, abs_ref, table_ref, gathered_ref,
):
    build_extended(old_ref, (h0, h1, h2, h3), ext_ref)
    tiles, width = rhs_ref.shape[0], rhs_ref.shape[2]
    chunks = width // LANES

    @pl.loop(0, tiles)
    def _(t):
        out = pull_and_solve(t, near_ref, count_ref, rhs_ref, inv_ref, cpl_ref, ext_ref, resid_ref)
        adj_ref[t] = out
        abs_ref[...] = jnp.abs(out)
        total = None
        for c in range(NVAR):
            term = hess_ref[t, c].astype(F32) * abs_ref[pl.ds(c, 1), :]
            total = term if total is None else total + term
        metric_ref[t] = total
        for q in range(chunks):
            table_ref[t * chunks + q, :NVAR, :] = total[:, q * LANES : (q + 1) * LANES]

    vertex = vertex_ref[...]
    entries = vertex.shape[1]
    groups = entries // LANES
    row = vertex // LANES
    lane = vertex % LANES
    rows_b = [jnp.broadcast_to(row[:, g * LANES : (g + 1) * LANES], (8, LANES)) for g in range(groups)]
    lanes_b = [jnp.broadcast_to(lane[:, g * LANES : (g + 1) * LANES], (8, LANES)) for g in range(groups)]

    def pick(r, totals):
        block = table_ref[r]
        return tuple(
            jnp.where(rows_b[g] == r, jnp.take_along_axis(block, lanes_b[g], axis=1), totals[g])
            for g in range(groups)
        )

    zero = jnp.zeros((8, LANES), F32)
    totals = lax.fori_loop(0, tiles * chunks, pick, (zero,) * groups, unroll=4)
    for g in range(groups):
        gathered_ref[:, g * LANES : (g + 1) * LANES] = totals[g]
    values = gathered_ref[...]
    which = lax.broadcasted_iota(jnp.int32, values.shape, 0)
    values = jnp.where(which == NVAR, slot_ref[...].astype(F32), jnp.where(which < NVAR, values, 0.0))
    high = values.astype(BF16).astype(F32)
    low = values - high

    regions = parcel_ref.shape[0]
    dest = region_ref[...]
    half = regions // 2

    for part in range(2):
        pieces = []
        for piece in (high, low):
            for d in range(half):
                pieces.append(jnp.where(dest == part * half + d, piece, 0.0))
        left = jnp.concatenate(pieces, axis=0).astype(BF16)
        placed = lax.dot_general(left, rank_hot_ref[...], (((1,), (1,)), ((), ())), preferred_element_type=F32)
        placed = placed[: half * 8] + placed[half * 8 :]
        for d in range(half):
            parcel_ref[part * half + d] = placed[d * 8 : (d + 1) * 8]


def rank_kernel(region_ref, hot_ref, rank_ref):
    entries = region_ref.shape[1]
    regions = 32
    upper = (
        lax.broadcasted_iota(jnp.int32, (LANES, LANES), 0) <= lax.broadcasted_iota(jnp.int32, (LANES, LANES), 1)
    )
    upper = jnp.where(upper, 1.0, 0.0).astype(BF16)
    region_id = lax.broadcasted_iota(jnp.int32, (regions, LANES), 0)
    carry = jnp.zeros((regions, 1), F32)
    for g in range(entries // LANES):
        here = region_id == region_ref[:, g * LANES : (g + 1) * LANES]
        hot = jnp.where(here, 1.0, 0.0)
        count = lax.dot_general(hot.astype(BF16), upper, (((1,), (0,)), ((), ())), preferred_element_type=F32) + carry
        rank_ref[:, g * LANES : (g + 1) * LANES] = jnp.sum(
            jnp.where(here, count - 1.0, 0.0), axis=0, keepdims=True
        )
        carry = count[:, LANES - 1 :]
    rank = rank_ref[...].astype(jnp.int32)
    places = lax.broadcasted_iota(jnp.int32, (CAP, entries), 0)
    hot_ref[...] = jnp.where(places == rank, 1.0, 0.0).astype(BF16)


def owner_kernel(parcel_ref, owned_ref):
    regions = parcel_ref.shape[0]
    highs = OWNED // LANES
    row_high = lax.broadcasted_iota(jnp.int32, (highs * 8, LANES), 0) // 8
    low_id = lax.broadcasted_iota(jnp.int32, (LANES, LANES), 0)
    total = jnp.zeros((2 * highs * 8, LANES), F32)
    for r in range(0, regions, 2):
        lefts, rights = [], []
        for q in (r, r + 1):
            block = parcel_ref[q]
            slot = block[NVAR : NVAR + 1, :].astype(jnp.int32)
            high = block.astype(BF16).astype(F32)
            low = block - high
            mask = row_high == slot // LANES
            tall_h = jnp.where(mask, jnp.concatenate([high] * highs, axis=0), 0.0)
            tall_l = jnp.where(mask, jnp.concatenate([low] * highs, axis=0), 0.0)
            lefts.append(jnp.concatenate([tall_h, tall_l], axis=0).astype(BF16))
            rights.append(jnp.where(low_id == slot % LANES, 1.0, 0.0).astype(BF16))
        left = jnp.concatenate(lefts, axis=1)
        right = jnp.concatenate(rights, axis=1)
        total += lax.dot_general(left, right, (((1,), (1,)), ((), ())), preferred_element_type=F32)
    total = total[: highs * 8] + total[highs * 8 :]
    for h in range(highs):
        owned_ref[:, h * LANES : (h + 1) * LANES] = total[h * 8 : h * 8 + NVAR]


def pairings(regions, subs):
    def swap(length, first):
        return [p for i in range(first, length - 1, 2) for p in ((i, i + 1), (i + 1, i))]

    along_region = [("region", swap(regions, 0)), ("region", swap(regions, 1))]
    along_sub = [("sub", swap(subs, 0)), ("sub", swap(subs, 1))]
    return along_region + along_sub


def exchange(sent):
    ra, rb, sa, sb = pairings(lax.axis_size("region"), lax.axis_size("sub"))
    got_rb = lax.ppermute(sent, *rb)
    got_ra = lax.ppermute(sent, *ra)
    got_sb = lax.ppermute(sent, *sb)
    got_sa = lax.ppermute(sent, *sa)
    return got_ra, got_rb, got_sa, got_sb


def per_device(
    rhs, diag_inv, coupling, neighbours, send_tiles, tile_count, hessian, shared_vertex, owner_region, owner_slot
):
    tiles, block, width = rhs.shape
    sends = send_tiles.shape[1]
    entries = shared_vertex.shape[0]
    regions = lax.axis_size("region")
    params = pltpu.CompilerParams(vmem_limit_bytes=40 * 2**20)
    near = pltpu.with_memory_space_constraint(coupling, pltpu.VMEM)
    coupling = near
    vertex = shared_vertex.reshape(1, entries)
    dest = owner_region.reshape(1, entries)
    slot = owner_slot.reshape(1, entries)

    adj_shape = jax.ShapeDtypeStruct((tiles * 8, width), F32)
    sent_shape = jax.ShapeDtypeStruct((sends * NVAR, width), F32)
    ext = pltpu.VMEM((tiles * 8 + 4 * sends * NVAR, width), F32)
    resid = pltpu.VMEM((8, width), F32)

    adjoint, sent = pl.pallas_call(
        first_kernel,
        out_shape=(adj_shape, sent_shape),
        in_specs=[SMEM, SMEM, VMEM, VMEM],
        out_specs=(VMEM, VMEM),
        compiler_params=params,
    )(send_tiles, tile_count, rhs, diag_inv)
    rank_hot = pl.pallas_call(
        rank_kernel,
        out_shape=jax.ShapeDtypeStruct((CAP, entries), BF16),
        in_specs=[VMEM],
        out_specs=VMEM,
        scratch_shapes=[pltpu.VMEM((1, entries), F32)],
        compiler_params=params,
    )(dest)
    for sweep in range(SWEEPS - 1):
        halos = exchange(sent)
        adjoint, sent = pl.pallas_call(
            sweep_kernel,
            out_shape=(adj_shape, sent_shape),
            in_specs=[SMEM] * 3 + [VMEM] * 8,
            out_specs=(VMEM, VMEM),
            scratch_shapes=[ext, resid],
            compiler_params=params,
        )(neighbours, send_tiles, tile_count, rhs, diag_inv, coupling, adjoint, *halos)
    halos = exchange(sent)
    out, metric, parcels = pl.pallas_call(
        last_kernel,
        out_shape=(
            jax.ShapeDtypeStruct((tiles, block, width), F32),
            jax.ShapeDtypeStruct((tiles, 6, width), F32),
            jax.ShapeDtypeStruct((regions, 8, CAP), F32),
        ),
        in_specs=[SMEM] * 2 + [VMEM] * 13,
        out_specs=(VMEM, VMEM, VMEM),
        scratch_shapes=[
            ext,
            resid,
            pltpu.VMEM((8, width), F32),
            pltpu.VMEM((tiles * width // LANES, 8, LANES), F32),
            pltpu.VMEM((8, entries), F32),
        ],
        compiler_params=params,
    )(neighbours, tile_count, rhs, diag_inv, coupling, hessian, adjoint, *halos, vertex, dest, slot, rank_hot)
    parcels = lax.all_to_all(parcels, "region", 0, 0, tiled=True)
    owned = pl.pallas_call(
        owner_kernel,
        out_shape=jax.ShapeDtypeStruct((6, OWNED), F32),
        in_specs=[VMEM],
        out_specs=VMEM,
        compiler_params=params,
    )(parcels)
    return out, metric, owned


def solution(mesh):
    both = ("region", "sub")
    placed = (
        P(both, None, None),
        P(both, None, None, None),
        P(both, None, None, None, None),
        P(both, None),
        P(both, None),
        P(both),
        P(both, None, None, None),
        P(both),
        P(both, None),
        P(both),
    )
    return jax.shard_map(
        per_device,
        mesh=mesh,
        in_specs=placed,
        out_specs=(P(both, None, None), P(both, None, None), P(None, both)),
        check_vma=False,
    )
```

```python
import functools

import jax
import jax.numpy as jnp
from jax import lax
from jax.experimental import pallas as pl
from jax.experimental.pallas import tpu as pltpu
from jax.sharding import PartitionSpec as P

NVAR = 6
SWEEPS = 3
OWNED = 1024
CAP = 128
LANES = 128

F32 = jnp.float32
BF16 = jnp.bfloat16

VMEM = pl.BlockSpec(memory_space=pltpu.VMEM)


def solve_tile(t, resid, inv_ref, live):
    total = None
    for j in range(inv_ref.shape[1]):
        term = inv_ref[t, j].astype(F32) * resid[pl.ds(j, 1), :]
        total = term if total is None else total + term
    rows = lax.broadcasted_iota(jnp.int32, total.shape, 0)
    return jnp.where((rows < NVAR) & live, total, 0.0)


def pack_sent(adj_ref, send_ref, sent_ref):
    for s in range(send_ref.shape[1]):
        tile = adj_ref[pl.ds(pl.multiple_of(send_ref[0, s] * 8, 8), 8), :]
        sent_ref[NVAR * s : NVAR * (s + 1), :] = tile[:NVAR]


def fetch(pairs, sems):
    copies = [pltpu.make_async_copy(src, dst, sems.at[i]) for i, (src, dst) in enumerate(pairs)]
    for copy in copies:
        copy.start()
    return copies


def first_kernel(
    send_hbm, count_ref, rhs_hbm, inv_hbm, adj_ref, sent_ref, rhs_ref, inv_ref, send_ref, sems, table_sems
):
    (send_copy,) = fetch(((send_hbm, send_ref),), table_sems)
    tiles = rhs_ref.shape[0]
    parts = sems.shape[0]
    step = tiles // parts
    copies = []
    for p in range(parts):
        some = pl.ds(p * step, step)
        copies.append(
            (
                pltpu.make_async_copy(rhs_hbm.at[some], rhs_ref.at[some], sems.at[p, 0]),
                pltpu.make_async_copy(inv_hbm.at[some], inv_ref.at[some], sems.at[p, 1]),
            )
        )
    for pair in copies:
        for copy in pair:
            copy.start()
    send_copy.wait()
    for p, pair in enumerate(copies):
        for copy in pair:
            copy.wait()

        @pl.loop(p * step, (p + 1) * step)
        def _(t):
            out = solve_tile(t, rhs_ref.at[t], inv_ref, t < count_ref[0])
            adj_ref[pl.ds(pl.multiple_of(t * 8, 8), 8), :] = out

    pack_sent(adj_ref, send_ref, sent_ref)


def build_extended(old_ref, halo_refs, ext_ref):
    own = old_ref.shape[0]
    ext_ref[:own, :] = old_ref[...]
    odd_region = lax.axis_index("region") % 2
    odd_sub = lax.axis_index("sub") % 2
    places = (3 - odd_sub, 1 - odd_region, 2 + odd_sub, odd_region)
    width = halo_refs[0].shape[0]
    for place, halo in zip(places, halo_refs):
        ext_ref[pl.ds(pl.multiple_of(own + place * width, 8), width), :] = halo[...]


def pull_and_solve(t, near_ref, count_ref, rhs_ref, inv_ref, cpl_ref, ext_ref, resid_ref):
    own = rhs_ref.shape[0]
    acc = rhs_ref[t]
    for k in range(cpl_ref.shape[1]):
        tile = near_ref[k, t]
        base = jnp.where(tile < own, tile * 8, tile * NVAR + own * (8 - NVAR))
        for m in range(NVAR):
            acc = acc - cpl_ref[t, k, m].astype(F32) * ext_ref[pl.ds(base + m, 1), :]
    resid_ref[...] = acc
    return solve_tile(t, resid_ref, inv_ref, t < count_ref[0])


def sweep_kernel(
    near_hbm, send_hbm, count_ref, rhs_ref, inv_ref, cpl_ref, old_ref, h0, h1, h2, h3,
    adj_ref, sent_ref, ext_ref, resid_ref, near_ref, send_ref, table_sems,
):
    tables = ((near_hbm, near_ref), (send_hbm, send_ref))
    copies = fetch(tables, table_sems)
    build_extended(old_ref, (h0, h1, h2, h3), ext_ref)
    for copy in copies:
        copy.wait()

    @pl.loop(0, rhs_ref.shape[0])
    def _(t):
        out = pull_and_solve(t, near_ref, count_ref, rhs_ref, inv_ref, cpl_ref, ext_ref, resid_ref)
        adj_ref[pl.ds(pl.multiple_of(t * 8, 8), 8), :] = out

    pack_sent(adj_ref, send_ref, sent_ref)


def sweep_load_kernel(
    near_hbm, send_hbm, count_ref, rhs_ref, inv_ref, cpl_hbm, old_ref, h0, h1, h2, h3,
    adj_ref, sent_ref, cpl_ref, ext_ref, resid_ref, near_ref, send_ref, table_sems, sems,
):
    tables = fetch(((near_hbm, near_ref), (send_hbm, send_ref)), table_sems)
    tiles = rhs_ref.shape[0]
    parts = sems.shape[0]
    step = tiles // parts
    copies = [
        pltpu.make_async_copy(
            cpl_hbm.at[pl.ds(p * step, step)], cpl_ref.at[pl.ds(p * step, step)], sems.at[p]
        )
        for p in range(parts)
    ]
    for copy in copies:
        copy.start()
    build_extended(old_ref, (h0, h1, h2, h3), ext_ref)
    for copy in tables:
        copy.wait()
    for p, copy in enumerate(copies):
        copy.wait()

        @pl.loop(p * step, (p + 1) * step)
        def _(t):
            out = pull_and_solve(t, near_ref, count_ref, rhs_ref, inv_ref, cpl_ref, ext_ref, resid_ref)
            adj_ref[pl.ds(pl.multiple_of(t * 8, 8), 8), :] = out

    pack_sent(adj_ref, send_ref, sent_ref)


def last_kernel(
    near_hbm, count_ref, rhs_ref, inv_ref, cpl_ref, hess_ref, old_ref, h0, h1, h2, h3,
    vertex_ref, region_ref, slot_ref, rank_hot_ref,
    adj_ref, metric_ref, parcel_ref, ext_ref, resid_ref, column_ref, gathered_ref, near_ref, table_sems,
):
    copies = fetch(((near_hbm, near_ref),), table_sems)
    build_extended(old_ref, (h0, h1, h2, h3), ext_ref)
    for copy in copies:
        copy.wait()
    tiles, width = rhs_ref.shape[0], rhs_ref.shape[2]
    chunks = width // LANES

    @pl.loop(0, tiles)
    def _(t):
        out = pull_and_solve(t, near_ref, count_ref, rhs_ref, inv_ref, cpl_ref, ext_ref, resid_ref)
        here = pl.ds(pl.multiple_of(t * 8, 8), 8)
        adj_ref[here, :] = out
        for q in range(chunks):
            column_ref[q, here, :] = jnp.abs(out[:, q * LANES : (q + 1) * LANES])

    for q in range(chunks):
        cols = slice(q * LANES, (q + 1) * LANES)
        sums = [None] * 6
        for c in range(NVAR):
            size = column_ref[q, pl.ds(c, tiles, stride=8), :]
            for s in range(6):
                term = hess_ref[c, s, :, cols].astype(F32) * size
                sums[s] = term if sums[s] is None else sums[s] + term
        for s in range(6):
            metric_ref[s, :, cols] = sums[s]

    entries = vertex_ref.shape[1]
    in_tile = lax.broadcasted_iota(jnp.int32, (8, LANES), 0)

    @pl.loop(0, entries // LANES)
    def _(g):
        here = pl.ds(pl.multiple_of(g * LANES, LANES), LANES)
        vertex = vertex_ref[:, here]
        row = jnp.broadcast_to(vertex // LANES, (8, LANES))
        lane = jnp.broadcast_to(vertex % LANES, (8, LANES))
        sums = [jnp.zeros((8, LANES), F32)] * 6
        for q in range(chunks):
            for h in range(tiles // 8):
                mine = row == (in_tile + h * 8) * chunks + q
                for s in range(6):
                    block = metric_ref[s, h * 8 : (h + 1) * 8, q * LANES : (q + 1) * LANES]
                    sums[s] = jnp.where(mine, jnp.take_along_axis(block, lane, axis=1), sums[s])
        for s in range(6):
            gathered_ref[s : s + 1, here] = jnp.sum(sums[s], axis=0, keepdims=True)

    values = gathered_ref[...]
    which = lax.broadcasted_iota(jnp.int32, values.shape, 0)
    values = jnp.where(which == NVAR, slot_ref[...].astype(F32), jnp.where(which < NVAR, values, 0.0))
    high = values.astype(BF16).astype(F32)
    low = values - high

    regions = parcel_ref.shape[0]
    dest = region_ref[...]
    half = regions // 2

    for part in range(2):
        pieces = []
        for piece in (high, low):
            for d in range(half):
                pieces.append(jnp.where(dest == part * half + d, piece, 0.0))
        left = jnp.concatenate(pieces, axis=0).astype(BF16)
        placed = lax.dot_general(left, rank_hot_ref[...], (((1,), (1,)), ((), ())), preferred_element_type=F32)
        placed = placed[: half * 8] + placed[half * 8 :]
        for d in range(half):
            parcel_ref[part * half + d] = placed[d * 8 : (d + 1) * 8]


def rank_kernel(region_ref, hot_ref, rank_ref):
    entries = region_ref.shape[1]
    regions = 32
    upper = (
        lax.broadcasted_iota(jnp.int32, (LANES, LANES), 0) <= lax.broadcasted_iota(jnp.int32, (LANES, LANES), 1)
    )
    upper = jnp.where(upper, 1.0, 0.0).astype(BF16)
    region_id = lax.broadcasted_iota(jnp.int32, (regions, LANES), 0)
    carry = jnp.zeros((regions, 1), F32)
    for g in range(entries // LANES):
        here = region_id == region_ref[:, g * LANES : (g + 1) * LANES]
        hot = jnp.where(here, 1.0, 0.0)
        count = lax.dot_general(hot.astype(BF16), upper, (((1,), (0,)), ((), ())), preferred_element_type=F32) + carry
        rank_ref[:, g * LANES : (g + 1) * LANES] = jnp.sum(
            jnp.where(here, count - 1.0, 0.0), axis=0, keepdims=True
        )
        carry = count[:, LANES - 1 :]
    rank = rank_ref[...].astype(jnp.int32)
    places = lax.broadcasted_iota(jnp.int32, (CAP, entries), 0)
    hot_ref[...] = jnp.where(places == rank, 1.0, 0.0).astype(BF16)


def owner_kernel(parcel_ref, owned_ref):
    regions = parcel_ref.shape[0]
    highs = OWNED // LANES
    row_high = lax.broadcasted_iota(jnp.int32, (highs * 8, LANES), 0) // 8
    low_id = lax.broadcasted_iota(jnp.int32, (LANES, LANES), 0)
    total = jnp.zeros((2 * highs * 8, LANES), F32)
    for r in range(0, regions, 2):
        lefts, rights = [], []
        for q in (r, r + 1):
            block = parcel_ref[q]
            slot = block[NVAR : NVAR + 1, :].astype(jnp.int32)
            high = block.astype(BF16).astype(F32)
            low = block - high
            mask = row_high == slot // LANES
            tall_h = jnp.where(mask, jnp.concatenate([high] * highs, axis=0), 0.0)
            tall_l = jnp.where(mask, jnp.concatenate([low] * highs, axis=0), 0.0)
            lefts.append(jnp.concatenate([tall_h, tall_l], axis=0).astype(BF16))
            rights.append(jnp.where(low_id == slot % LANES, 1.0, 0.0).astype(BF16))
        left = jnp.concatenate(lefts, axis=1)
        right = jnp.concatenate(rights, axis=1)
        total += lax.dot_general(left, right, (((1,), (1,)), ((), ())), preferred_element_type=F32)
    total = total[: highs * 8] + total[highs * 8 :]
    for h in range(highs):
        owned_ref[:, h * LANES : (h + 1) * LANES] = total[h * 8 : h * 8 + NVAR]


def pairings(regions, subs):
    def swap(length, first):
        return [p for i in range(first, length - 1, 2) for p in ((i, i + 1), (i + 1, i))]

    along_region = [("region", swap(regions, 0)), ("region", swap(regions, 1))]
    along_sub = [("sub", swap(subs, 0)), ("sub", swap(subs, 1))]
    return along_region + along_sub


def exchange(sent):
    ra, rb, sa, sb = pairings(lax.axis_size("region"), lax.axis_size("sub"))
    got_rb = lax.ppermute(sent, *rb)
    got_ra = lax.ppermute(sent, *ra)
    got_sb = lax.ppermute(sent, *sb)
    got_sa = lax.ppermute(sent, *sa)
    return got_sa, got_ra, got_sb, got_rb


def per_device(
    rhs, diag_inv, coupling, neighbours, send_tiles, tile_count, hessian, shared_vertex, owner_region, owner_slot
):
    tiles, block, width = rhs.shape
    sends = send_tiles.shape[1]
    entries = shared_vertex.shape[0]
    regions = lax.axis_size("region")
    params = pltpu.CompilerParams(vmem_limit_bytes=40 * 2**20)
    rhs = pltpu.with_memory_space_constraint(rhs, pltpu.HBM)
    diag_inv = pltpu.with_memory_space_constraint(diag_inv, pltpu.HBM)
    coupling = pltpu.with_memory_space_constraint(coupling, pltpu.HBM)
    neighbours = pltpu.with_memory_space_constraint(neighbours.T, pltpu.HBM)
    send_tiles = pltpu.with_memory_space_constraint(send_tiles, pltpu.HBM)
    vertex = shared_vertex.reshape(1, entries)
    dest = owner_region.reshape(1, entries)
    slot = owner_slot.reshape(1, entries)

    adj_shape = jax.ShapeDtypeStruct((tiles * 8, width), F32)
    sent_shape = jax.ShapeDtypeStruct((sends * NVAR, width), F32)
    ext = pltpu.VMEM((tiles * 8 + 4 * sends * NVAR, width), F32)
    resid = pltpu.VMEM((8, width), F32)
    hbm = pl.BlockSpec(memory_space=pltpu.HBM)
    smem = pl.BlockSpec(memory_space=pltpu.SMEM)
    near_table = pltpu.SMEM(neighbours.shape, jnp.int32)
    send_table = pltpu.SMEM(send_tiles.shape, jnp.int32)

    adjoint, sent, rhs, diag_inv = pl.pallas_call(
        first_kernel,
        out_shape=(
            adj_shape,
            sent_shape,
            jax.ShapeDtypeStruct(rhs.shape, rhs.dtype),
            jax.ShapeDtypeStruct(diag_inv.shape, diag_inv.dtype),
        ),
        in_specs=[hbm, smem, hbm, hbm],
        out_specs=(VMEM,) * 4,
        scratch_shapes=[send_table, pltpu.SemaphoreType.DMA((4, 2)), pltpu.SemaphoreType.DMA((1,))],
        compiler_params=params,
    )(send_tiles, tile_count, rhs, diag_inv)
    rank_hot = pl.pallas_call(
        rank_kernel,
        out_shape=jax.ShapeDtypeStruct((CAP, entries), BF16),
        in_specs=[VMEM],
        out_specs=VMEM,
        scratch_shapes=[pltpu.VMEM((1, entries), F32)],
        compiler_params=params,
    )(dest)
    halos = exchange(sent)
    adjoint, sent, coupling = pl.pallas_call(
        sweep_load_kernel,
        out_shape=(adj_shape, sent_shape, jax.ShapeDtypeStruct(coupling.shape, coupling.dtype)),
        in_specs=[hbm, hbm, smem] + [VMEM] * 2 + [hbm] + [VMEM] * 5,
        out_specs=(VMEM,) * 3,
        scratch_shapes=[
            ext, resid, near_table, send_table,
            pltpu.SemaphoreType.DMA((2,)), pltpu.SemaphoreType.DMA((8,)),
        ],
        compiler_params=params,
    )(neighbours, send_tiles, tile_count, rhs, diag_inv, coupling, adjoint, *halos)
    for sweep in range(SWEEPS - 2):
        halos = exchange(sent)
        adjoint, sent = pl.pallas_call(
            sweep_kernel,
            out_shape=(adj_shape, sent_shape),
            in_specs=[hbm, hbm, smem] + [VMEM] * 8,
            out_specs=(VMEM, VMEM),
            scratch_shapes=[ext, resid, near_table, send_table, pltpu.SemaphoreType.DMA((2,))],
            compiler_params=params,
        )(neighbours, send_tiles, tile_count, rhs, diag_inv, coupling, adjoint, *halos)
    halos = exchange(sent)
    out, metric, parcels = pl.pallas_call(
        last_kernel,
        out_shape=(
            adj_shape,
            jax.ShapeDtypeStruct((6, tiles, width), F32),
            jax.ShapeDtypeStruct((regions, 8, CAP), F32),
        ),
        in_specs=[hbm, smem] + [VMEM] * 13,
        out_specs=(VMEM, VMEM, VMEM),
        scratch_shapes=[
            ext,
            resid,
            pltpu.VMEM((width // LANES, tiles * 8, LANES), F32),
            pltpu.VMEM((8, entries), F32),
            near_table,
            pltpu.SemaphoreType.DMA((1,)),
        ],
        compiler_params=params,
    )(
        neighbours, tile_count, rhs, diag_inv, coupling, hessian.transpose(1, 2, 0, 3), adjoint, *halos,
        vertex, dest, slot, rank_hot,
    )
    out = out.reshape(tiles, block, width)
    metric = metric.transpose(1, 0, 2)
    parcels = lax.all_to_all(parcels, "region", 0, 0, tiled=True)
    owned = pl.pallas_call(
        owner_kernel,
        out_shape=jax.ShapeDtypeStruct((6, OWNED), F32),
        in_specs=[VMEM],
        out_specs=VMEM,
        compiler_params=params,
    )(parcels)
    return out, metric, owned


def solution(mesh):
    both = ("region", "sub")
    placed = (
        P(both, None, None),
        P(both, None, None, None),
        P(both, None, None, None, None),
        P(both, None),
        P(both, None),
        P(both),
        P(both, None, None, None),
        P(both),
        P(both, None),
        P(both),
    )
    return jax.shard_map(
        per_device,
        mesh=mesh,
        in_specs=placed,
        out_specs=(P(both, None, None), P(both, None, None), P(None, both)),
        check_vma=False,
    )
```

```python
import functools

import jax
import jax.numpy as jnp
from jax import lax
from jax.experimental import pallas as pl
from jax.experimental.pallas import tpu as pltpu
from jax.sharding import PartitionSpec as P

NVAR = 6
SWEEPS = 3
OWNED = 1024
CAP = 128
LANES = 128

F32 = jnp.float32
BF16 = jnp.bfloat16

VMEM = pl.BlockSpec(memory_space=pltpu.VMEM)


def lanes_of(q):
    return slice(q * LANES, (q + 1) * LANES)


def rows_of(t):
    return pl.ds(pl.multiple_of(t * 8, 8), 8)


def solve_tile(t, row_of, inv_ref, live):
    keep = (lax.broadcasted_iota(jnp.int32, (8, LANES), 0) < NVAR) & live
    blocks = []
    for q in range(inv_ref.shape[3] // LANES):
        total = None
        for j in range(inv_ref.shape[1]):
            term = inv_ref[t, j, :, lanes_of(q)].astype(F32) * row_of(q, j)
            total = term if total is None else total + term
        blocks.append(jnp.where(keep, total, 0.0))
    return blocks


def pack_sent(adj_ref, send_ref, sent_ref):
    for s in range(send_ref.shape[1]):
        here = rows_of(send_ref[0, s])
        for q in range(adj_ref.shape[0]):
            sent_ref[q, NVAR * s : NVAR * (s + 1), :] = adj_ref[q, here, :][:NVAR]


def fetch(pairs, sems):
    copies = [pltpu.make_async_copy(src, dst, sems.at[i]) for i, (src, dst) in enumerate(pairs)]
    for copy in copies:
        copy.start()
    return copies


def first_kernel(send_hbm, count_ref, rhs_hbm, inv_hbm, adj_ref, sent_ref, rhs_ref, inv_ref, send_ref, sems, table_sems):
    (send_copy,) = fetch(((send_hbm, send_ref),), table_sems)
    tiles = rhs_ref.shape[0]
    parts = sems.shape[0]
    step = tiles // parts
    copies = []
    for p in range(parts):
        some = pl.ds(p * step, step)
        copies.append(
            (
                pltpu.make_async_copy(rhs_hbm.at[some], rhs_ref.at[some], sems.at[p, 0]),
                pltpu.make_async_copy(inv_hbm.at[some], inv_ref.at[some], sems.at[p, 1]),
            )
        )
    for pair in copies:
        for copy in pair:
            copy.start()
    send_copy.wait()
    for p, pair in enumerate(copies):
        for copy in pair:
            copy.wait()

        @pl.loop(p * step, (p + 1) * step)
        def _(t):
            blocks = solve_tile(t, lambda q, j: rhs_ref[t, j : j + 1, lanes_of(q)], inv_ref, t < count_ref[0])
            for q, block in enumerate(blocks):
                adj_ref[q, rows_of(t), :] = block

    pack_sent(adj_ref, send_ref, sent_ref)


def load_kernel(cpl_hbm, cpl_ref, sems):
    parts = sems.shape[0]
    step = cpl_ref.shape[0] // parts
    some = [pl.ds(p * step, step) for p in range(parts)]
    for copy in fetch([(cpl_hbm.at[s], cpl_ref.at[s]) for s in some], sems):
        copy.wait()


def build_extended(old_ref, halo_refs, ext_ref):
    own = old_ref.shape[1]
    ext_ref[:, :own, :] = old_ref[...]
    odd_region = lax.axis_index("region") % 2
    odd_sub = lax.axis_index("sub") % 2
    places = (2 + odd_sub, 1 - odd_region, odd_region, 3 - odd_sub)
    width = halo_refs[0].shape[1]
    for place, halo in zip(places, halo_refs):
        ext_ref[:, pl.ds(pl.multiple_of(own + place * width, 8), width), :] = halo[...]


def sweep_tiles(near_ref, count_ref, rhs_ref, inv_ref, cpl_ref, ext_ref, resid_ref, put):
    own = rhs_ref.shape[0]

    @pl.loop(0, own)
    def _(t):
        bases = []
        for k in range(cpl_ref.shape[1]):
            tile = near_ref[k, t]
            bases.append(jnp.where(tile < own, tile * 8, tile * NVAR + own * (8 - NVAR)))
        for q in range(resid_ref.shape[0]):
            sums = [rhs_ref[t, :, lanes_of(q)], None]
            for k, base in enumerate(bases):
                for m in range(NVAR):
                    term = cpl_ref[t, k, m, :, lanes_of(q)].astype(F32) * ext_ref[q, pl.ds(base + m, 1), :]
                    if k % 2:
                        sums[1] = term if sums[1] is None else sums[1] + term
                    else:
                        sums[0] = sums[0] - term
            resid_ref[q] = sums[0] - sums[1]
        put(t, solve_tile(t, lambda q, j: resid_ref[q, j : j + 1, :], inv_ref, t < count_ref[0]))


def sweep_kernel(
    near_hbm, send_hbm, count_ref, rhs_ref, inv_ref, cpl_ref, old_ref, h0, h1, h2, h3,
    adj_ref, sent_ref, ext_ref, resid_ref, near_ref, send_ref, table_sems,
):
    copies = fetch(((near_hbm, near_ref), (send_hbm, send_ref)), table_sems)
    build_extended(old_ref, (h0, h1, h2, h3), ext_ref)
    for copy in copies:
        copy.wait()

    def put(t, blocks):
        for q, block in enumerate(blocks):
            adj_ref[q, rows_of(t), :] = block

    sweep_tiles(near_ref, count_ref, rhs_ref, inv_ref, cpl_ref, ext_ref, resid_ref, put)
    pack_sent(adj_ref, send_ref, sent_ref)


def last_kernel(
    near_hbm, count_ref, rhs_ref, inv_ref, cpl_ref, hess_ref, old_ref, h0, h1, h2, h3,
    vertex_ref, region_ref, slot_ref, rank_hot_ref,
    adj_hbm, metric_hbm, parcel_ref,
    ext_ref, resid_ref, adj_ref, metric_ref, column_ref, gathered_ref, near_ref, table_sems, out_sems,
):
    copies = fetch(((near_hbm, near_ref),), table_sems)
    build_extended(old_ref, (h0, h1, h2, h3), ext_ref)
    for copy in copies:
        copy.wait()
    tiles, width = rhs_ref.shape[0], rhs_ref.shape[2]
    chunks = width // LANES

    def put(t, blocks):
        for q, block in enumerate(blocks):
            adj_ref[rows_of(t), lanes_of(q)] = block
            column_ref[q, rows_of(t), :] = jnp.abs(block)

    sweep_tiles(near_ref, count_ref, rhs_ref, inv_ref, cpl_ref, ext_ref, resid_ref, put)
    adj_out = pltpu.make_async_copy(adj_ref, adj_hbm, out_sems.at[0])
    adj_out.start()

    for q in range(chunks):
        sums = [None] * 6
        for c in range(NVAR):
            size = column_ref[q, pl.ds(c, tiles, stride=8), :]
            for s in range(6):
                term = hess_ref[c, s, :, lanes_of(q)].astype(F32) * size
                sums[s] = term if sums[s] is None else sums[s] + term
        for s in range(6):
            metric_ref[s, :, lanes_of(q)] = sums[s]
    metric_out = pltpu.make_async_copy(metric_ref, metric_hbm, out_sems.at[1])
    metric_out.start()

    entries = vertex_ref.shape[1]
    in_tile = lax.broadcasted_iota(jnp.int32, (8, LANES), 0)

    @pl.loop(0, entries // LANES)
    def _(g):
        here = pl.ds(pl.multiple_of(g * LANES, LANES), LANES)
        vertex = vertex_ref[:, here]
        row = jnp.broadcast_to(vertex // LANES, (8, LANES))
        lane = jnp.broadcast_to(vertex % LANES, (8, LANES))
        sums = [jnp.zeros((8, LANES), F32)] * 6
        for q in range(chunks):
            for h in range(tiles // 8):
                mine = row == (in_tile + h * 8) * chunks + q
                for s in range(6):
                    block = metric_ref[s, h * 8 : (h + 1) * 8, q * LANES : (q + 1) * LANES]
                    sums[s] = jnp.where(mine, jnp.take_along_axis(block, lane, axis=1), sums[s])
        for s in range(6):
            gathered_ref[s : s + 1, here] = jnp.sum(sums[s], axis=0, keepdims=True)

    values = gathered_ref[...]
    which = lax.broadcasted_iota(jnp.int32, values.shape, 0)
    values = jnp.where(which == NVAR, slot_ref[...].astype(F32), jnp.where(which < NVAR, values, 0.0))
    high = values.astype(BF16).astype(F32)
    low = values - high

    regions = parcel_ref.shape[0]
    dest = region_ref[...]
    half = regions // 2

    for part in range(2):
        pieces = []
        for piece in (high, low):
            for d in range(half):
                pieces.append(jnp.where(dest == part * half + d, piece, 0.0))
        left = jnp.concatenate(pieces, axis=0).astype(BF16)
        placed = lax.dot_general(left, rank_hot_ref[...], (((1,), (1,)), ((), ())), preferred_element_type=F32)
        placed = placed[: half * 8] + placed[half * 8 :]
        for d in range(half):
            parcel_ref[part * half + d] = placed[d * 8 : (d + 1) * 8]
    adj_out.wait()
    metric_out.wait()


def rank_kernel(region_ref, hot_ref, rank_ref):
    entries = region_ref.shape[1]
    regions = 32
    upper = (
        lax.broadcasted_iota(jnp.int32, (LANES, LANES), 0) <= lax.broadcasted_iota(jnp.int32, (LANES, LANES), 1)
    )
    upper = jnp.where(upper, 1.0, 0.0).astype(BF16)
    region_id = lax.broadcasted_iota(jnp.int32, (regions, LANES), 0)
    carry = jnp.zeros((regions, 1), F32)
    for g in range(entries // LANES):
        here = region_id == region_ref[:, g * LANES : (g + 1) * LANES]
        hot = jnp.where(here, 1.0, 0.0)
        count = lax.dot_general(hot.astype(BF16), upper, (((1,), (0,)), ((), ())), preferred_element_type=F32) + carry
        rank_ref[:, g * LANES : (g + 1) * LANES] = jnp.sum(
            jnp.where(here, count - 1.0, 0.0), axis=0, keepdims=True
        )
        carry = count[:, LANES - 1 :]
    rank = rank_ref[...].astype(jnp.int32)
    places = lax.broadcasted_iota(jnp.int32, (CAP, entries), 0)
    hot_ref[...] = jnp.where(places == rank, 1.0, 0.0).astype(BF16)


def owner_kernel(parcel_ref, owned_ref):
    regions = parcel_ref.shape[0]
    highs = OWNED // LANES
    row_high = lax.broadcasted_iota(jnp.int32, (highs * 8, LANES), 0) // 8
    low_id = lax.broadcasted_iota(jnp.int32, (LANES, LANES), 0)
    total = jnp.zeros((2 * highs * 8, LANES), F32)
    for r in range(0, regions, 2):
        lefts, rights = [], []
        for q in (r, r + 1):
            block = parcel_ref[q]
            slot = block[NVAR : NVAR + 1, :].astype(jnp.int32)
            high = block.astype(BF16).astype(F32)
            low = block - high
            mask = row_high == slot // LANES
            tall_h = jnp.where(mask, jnp.concatenate([high] * highs, axis=0), 0.0)
            tall_l = jnp.where(mask, jnp.concatenate([low] * highs, axis=0), 0.0)
            lefts.append(jnp.concatenate([tall_h, tall_l], axis=0).astype(BF16))
            rights.append(jnp.where(low_id == slot % LANES, 1.0, 0.0).astype(BF16))
        left = jnp.concatenate(lefts, axis=1)
        right = jnp.concatenate(rights, axis=1)
        total += lax.dot_general(left, right, (((1,), (1,)), ((), ())), preferred_element_type=F32)
    total = total[: highs * 8] + total[highs * 8 :]
    for h in range(highs):
        owned_ref[:, h * LANES : (h + 1) * LANES] = total[h * 8 : h * 8 + NVAR]


def pairings(regions, subs):
    def swap(length, first):
        return [p for i in range(first, length - 1, 2) for p in ((i, i + 1), (i + 1, i))]

    along_region = [("region", swap(regions, 0)), ("region", swap(regions, 1))]
    along_sub = [("sub", swap(subs, 0)), ("sub", swap(subs, 1))]
    return along_region + along_sub


def exchange(sent):
    ra, rb, sa, sb = pairings(lax.axis_size("region"), lax.axis_size("sub"))
    got_rb = lax.ppermute(sent, *rb)
    got_ra = lax.ppermute(sent, *ra)
    got_sb = lax.ppermute(sent, *sb)
    got_sa = lax.ppermute(sent, *sa)
    return got_sb, got_ra, got_rb, got_sa


def per_device(
    rhs, diag_inv, coupling, neighbours, send_tiles, tile_count, hessian, shared_vertex, owner_region, owner_slot
):
    tiles, block, width = rhs.shape
    sends = send_tiles.shape[1]
    entries = shared_vertex.shape[0]
    regions = lax.axis_size("region")
    params = pltpu.CompilerParams(vmem_limit_bytes=40 * 2**20)
    rhs = pltpu.with_memory_space_constraint(rhs, pltpu.HBM)
    diag_inv = pltpu.with_memory_space_constraint(diag_inv, pltpu.HBM)
    coupling = pltpu.with_memory_space_constraint(coupling, pltpu.HBM)
    neighbours = pltpu.with_memory_space_constraint(neighbours.T, pltpu.HBM)
    send_tiles = pltpu.with_memory_space_constraint(send_tiles, pltpu.HBM)
    vertex = shared_vertex.reshape(1, entries)
    dest = owner_region.reshape(1, entries)
    slot = owner_slot.reshape(1, entries)

    chunks = width // LANES
    adj_shape = jax.ShapeDtypeStruct((chunks, tiles * 8, LANES), F32)
    sent_shape = jax.ShapeDtypeStruct((chunks, sends * NVAR, LANES), F32)
    ext = pltpu.VMEM((chunks, tiles * 8 + 4 * sends * NVAR, LANES), F32)
    resid = pltpu.VMEM((chunks, 8, LANES), F32)
    hbm = pl.BlockSpec(memory_space=pltpu.HBM)
    smem = pl.BlockSpec(memory_space=pltpu.SMEM)
    near_table = pltpu.SMEM(neighbours.shape, jnp.int32)
    send_table = pltpu.SMEM(send_tiles.shape, jnp.int32)

    adjoint, sent, rhs, diag_inv = pl.pallas_call(
        first_kernel,
        out_shape=(
            adj_shape,
            sent_shape,
            jax.ShapeDtypeStruct(rhs.shape, rhs.dtype),
            jax.ShapeDtypeStruct(diag_inv.shape, diag_inv.dtype),
        ),
        in_specs=[hbm, smem, hbm, hbm],
        out_specs=(VMEM,) * 4,
        scratch_shapes=[send_table, pltpu.SemaphoreType.DMA((4, 2)), pltpu.SemaphoreType.DMA((1,))],
        compiler_params=params,
        name="first",
    )(send_tiles, tile_count, rhs, diag_inv)
    coupling = pl.pallas_call(
        load_kernel,
        out_shape=jax.ShapeDtypeStruct(coupling.shape, coupling.dtype),
        in_specs=[hbm],
        out_specs=VMEM,
        scratch_shapes=[pltpu.SemaphoreType.DMA((4,))],
        compiler_params=params,
        cost_estimate=pl.CostEstimate(flops=0, bytes_accessed=2 * coupling.size * 2, transcendentals=0),
        name="load",
    )(coupling)
    rank_hot = pl.pallas_call(
        rank_kernel,
        out_shape=jax.ShapeDtypeStruct((CAP, entries), BF16),
        in_specs=[VMEM],
        out_specs=VMEM,
        scratch_shapes=[pltpu.VMEM((1, entries), F32)],
        compiler_params=params,
        name="rank",
    )(dest)
    for sweep in range(SWEEPS - 1):
        halos = exchange(sent)
        adjoint, sent = pl.pallas_call(
            sweep_kernel,
            out_shape=(adj_shape, sent_shape),
            in_specs=[hbm, hbm, smem] + [VMEM] * 8,
            out_specs=(VMEM, VMEM),
            scratch_shapes=[ext, resid, near_table, send_table, pltpu.SemaphoreType.DMA((2,))],
            compiler_params=params,
            name="sweep",
        )(neighbours, send_tiles, tile_count, rhs, diag_inv, coupling, adjoint, *halos)
    halos = exchange(sent)
    out, metric, parcels = pl.pallas_call(
        last_kernel,
        out_shape=(
            jax.ShapeDtypeStruct((tiles * 8, width), F32),
            jax.ShapeDtypeStruct((6, tiles, width), F32),
            jax.ShapeDtypeStruct((regions, 8, CAP), F32),
        ),
        in_specs=[hbm, smem] + [VMEM] * 13,
        out_specs=(hbm, hbm, VMEM),
        scratch_shapes=[
            ext,
            resid,
            pltpu.VMEM((tiles * 8, width), F32),
            pltpu.VMEM((6, tiles, width), F32),
            pltpu.VMEM((chunks, tiles * 8, LANES), F32),
            pltpu.VMEM((8, entries), F32),
            near_table,
            pltpu.SemaphoreType.DMA((1,)),
            pltpu.SemaphoreType.DMA((2,)),
        ],
        compiler_params=params,
        name="last",
    )(
        neighbours, tile_count, rhs, diag_inv, coupling, hessian.transpose(1, 2, 0, 3), adjoint, *halos,
        vertex, dest, slot, rank_hot,
    )
    out = out.reshape(tiles, block, width)
    metric = metric.transpose(1, 0, 2)
    parcels = lax.all_to_all(parcels, "region", 0, 0, tiled=True)
    owned = pl.pallas_call(
        owner_kernel,
        out_shape=jax.ShapeDtypeStruct((6, OWNED), F32),
        in_specs=[VMEM],
        out_specs=VMEM,
        compiler_params=params,
        name="owner",
    )(parcels)
    return out, metric, owned


def solution(mesh):
    both = ("region", "sub")
    placed = (
        P(both, None, None),
        P(both, None, None, None),
        P(both, None, None, None, None),
        P(both, None),
        P(both, None),
        P(both),
        P(both, None, None, None),
        P(both),
        P(both, None),
        P(both),
    )
    return jax.shard_map(
        per_device,
        mesh=mesh,
        in_specs=placed,
        out_specs=(P(both, None, None), P(both, None, None), P(None, both)),
        check_vma=False,
    )
```

```python
import functools

import jax
import jax.numpy as jnp
from jax import lax
from jax.experimental import pallas as pl
from jax.experimental.pallas import tpu as pltpu
from jax.sharding import PartitionSpec as P

NVAR = 6
SWEEPS = 3
OWNED = 1024
CAP = 128
LANES = 128

ORDER = ("sa", "rb", "ra", "sb")
LAST_ORDER = ("ra", "sb", "sa", "rb")

F32 = jnp.float32
BF16 = jnp.bfloat16

VMEM = pl.BlockSpec(memory_space=pltpu.VMEM)


def lanes_of(q):
    return slice(q * LANES, (q + 1) * LANES)


def rows_of(t):
    return pl.ds(pl.multiple_of(t * 8, 8), 8)


def solve_tile(t, row_of, inv_ref, live):
    keep = (lax.broadcasted_iota(jnp.int32, (8, LANES), 0) < NVAR) & live
    blocks = []
    for q in range(inv_ref.shape[3] // LANES):
        total = None
        for j in range(inv_ref.shape[1]):
            term = inv_ref[t, j, :, lanes_of(q)].astype(F32) * row_of(q, j)
            total = term if total is None else total + term
        blocks.append(jnp.where(keep, total, 0.0))
    return blocks


def pack_sent(adj_ref, send_ref, sent_ref):
    for s in range(send_ref.shape[1]):
        here = rows_of(send_ref[0, s])
        for q in range(adj_ref.shape[0]):
            sent_ref[q, NVAR * s : NVAR * (s + 1), :] = adj_ref[q, here, :][:NVAR]


def fetch(pairs, sems):
    copies = [pltpu.make_async_copy(src, dst, sems.at[i]) for i, (src, dst) in enumerate(pairs)]
    for copy in copies:
        copy.start()
    return copies


def put_rows(adj_ref, t, blocks):
    for q, block in enumerate(blocks):
        adj_ref[q, rows_of(t), :] = block


def first_kernel(
    send_hbm, near_hbm, count_ref, rhs_hbm, inv_hbm,
    adj_ref, sent_ref, rhs_ref, inv_ref, send_ref, near_ref, listed_ref, sems, table_sems,
):
    send_copy, near_copy = fetch(((send_hbm, send_ref), (near_hbm, near_ref)), table_sems)
    tiles, sends = rhs_ref.shape[0], send_ref.shape[1]
    half = tiles // 2
    pairs = [(rhs_hbm, rhs_ref)]
    pairs += [(inv_hbm.at[pl.ds(p * half, half)], inv_ref.at[pl.ds(p * half, half)]) for p in range(2)]
    copies = fetch(pairs, sems)
    send_copy.wait()
    for t in range(tiles):
        listed_ref[0, t] = 0
    for s in range(sends):
        listed_ref[0, send_ref[0, s]] = 1
    for copy in copies:
        copy.wait()

    @pl.loop(0, sends)
    def _(s):
        t = send_ref[0, s]
        row_of = lambda q, j: rhs_ref[t, j : j + 1, lanes_of(q)]
        put_rows(adj_ref, t, solve_tile(t, row_of, inv_ref, t < count_ref[0]))

    pack_sent(adj_ref, send_ref, sent_ref)
    near_copy.wait()


def first_rest_kernel(listed_ref, count_ref, rhs_ref, inv_ref, lead_ref, cpl_hbm, adj_ref, cpl_ref, sems):
    parts = sems.shape[0]
    step = cpl_ref.shape[0] // parts
    some = [pl.ds(p * step, step) for p in range(parts)]
    copies = fetch([(cpl_hbm.at[s], cpl_ref.at[s]) for s in some], sems)
    adj_ref[...] = lead_ref[...]

    @pl.loop(0, rhs_ref.shape[0])
    def _(t):
        @pl.when(listed_ref[0, t] == 0)
        def _():
            row_of = lambda q, j: rhs_ref[t, j : j + 1, lanes_of(q)]
            put_rows(adj_ref, t, solve_tile(t, row_of, inv_ref, t < count_ref[0]))

    for copy in copies:
        copy.wait()


def build_extended(order, old_ref, halo_refs, ext_ref):
    own = old_ref.shape[1]
    ext_ref[:, :own, :] = old_ref[...]
    odd_region = lax.axis_index("region") % 2
    odd_sub = lax.axis_index("sub") % 2
    places = {"ra": 1 - odd_region, "rb": odd_region, "sa": 3 - odd_sub, "sb": 2 + odd_sub}
    width = halo_refs[0].shape[1]
    for name, halo in zip(order, halo_refs):
        ext_ref[:, pl.ds(pl.multiple_of(own + places[name] * width, 8), width), :] = halo[...]


def sweep_tile(t, near_ref, count_ref, rhs_ref, inv_ref, cpl_ref, ext_ref, resid_ref):
    own = rhs_ref.shape[0]
    bases = []
    for k in range(cpl_ref.shape[1]):
        tile = near_ref[k, t]
        bases.append(jnp.where(tile < own, tile * 8, tile * NVAR + own * (8 - NVAR)))
    for q in range(resid_ref.shape[0]):
        sums = [rhs_ref[t, :, lanes_of(q)], None]
        for k, base in enumerate(bases):
            for m in range(NVAR):
                term = cpl_ref[t, k, m, :, lanes_of(q)].astype(F32) * ext_ref[q, pl.ds(base + m, 1), :]
                if k % 2:
                    sums[1] = term if sums[1] is None else sums[1] + term
                else:
                    sums[0] = sums[0] - term
        resid_ref[q] = sums[0] - sums[1]
    return solve_tile(t, lambda q, j: resid_ref[q, j : j + 1, :], inv_ref, t < count_ref[0])


def lead_kernel(
    order, near_ref, send_ref, count_ref, rhs_ref, inv_ref, cpl_ref, old_ref, h0, h1, h2, h3,
    adj_ref, sent_ref, ext_ref, resid_ref,
):
    build_extended(order, old_ref, (h0, h1, h2, h3), ext_ref)

    @pl.loop(0, send_ref.shape[1])
    def _(s):
        t = send_ref[0, s]
        put_rows(adj_ref, t, sweep_tile(t, near_ref, count_ref, rhs_ref, inv_ref, cpl_ref, ext_ref, resid_ref))

    pack_sent(adj_ref, send_ref, sent_ref)


def rest_kernel(
    near_ref, listed_ref, count_ref, rhs_ref, inv_ref, cpl_ref, ext_ref, lead_ref, adj_ref, resid_ref
):
    adj_ref[...] = lead_ref[...]

    @pl.loop(0, rhs_ref.shape[0])
    def _(t):
        @pl.when(listed_ref[0, t] == 0)
        def _():
            put_rows(adj_ref, t, sweep_tile(t, near_ref, count_ref, rhs_ref, inv_ref, cpl_ref, ext_ref, resid_ref))


def last_kernel(
    order, near_ref, count_ref, rhs_ref, inv_ref, cpl_ref, hess_ref, old_ref, h0, h1, h2, h3,
    vertex_ref, region_ref, slot_ref, rank_hot_ref,
    adj_hbm, metric_hbm, parcel_ref,
    ext_ref, resid_ref, adj_ref, metric_ref, column_ref, gathered_ref, out_sems,
):
    build_extended(order, old_ref, (h0, h1, h2, h3), ext_ref)
    tiles, width = rhs_ref.shape[0], rhs_ref.shape[2]
    chunks = width // LANES

    @pl.loop(0, tiles)
    def _(t):
        blocks = sweep_tile(t, near_ref, count_ref, rhs_ref, inv_ref, cpl_ref, ext_ref, resid_ref)
        for q, block in enumerate(blocks):
            adj_ref[rows_of(t), lanes_of(q)] = block
            column_ref[q, rows_of(t), :] = jnp.abs(block)

    adj_out = pltpu.make_async_copy(adj_ref, adj_hbm, out_sems.at[0])
    adj_out.start()

    for q in range(chunks):
        sums = [None] * 6
        for c in range(NVAR):
            size = column_ref[q, pl.ds(c, tiles, stride=8), :]
            for s in range(6):
                term = hess_ref[c, s, :, lanes_of(q)].astype(F32) * size
                sums[s] = term if sums[s] is None else sums[s] + term
        for s in range(6):
            metric_ref[s, :, lanes_of(q)] = sums[s]
    metric_out = pltpu.make_async_copy(metric_ref, metric_hbm, out_sems.at[1])
    metric_out.start()

    entries = vertex_ref.shape[1]
    in_tile = lax.broadcasted_iota(jnp.int32, (8, LANES), 0)

    @pl.loop(0, entries // LANES)
    def _(g):
        here = pl.ds(pl.multiple_of(g * LANES, LANES), LANES)
        vertex = vertex_ref[:, here]
        row = jnp.broadcast_to(vertex // LANES, (8, LANES))
        lane = jnp.broadcast_to(vertex % LANES, (8, LANES))
        sums = [jnp.zeros((8, LANES), F32)] * 6
        for q in range(chunks):
            for h in range(tiles // 8):
                mine = row == (in_tile + h * 8) * chunks + q
                for s in range(6):
                    block = metric_ref[s, h * 8 : (h + 1) * 8, q * LANES : (q + 1) * LANES]
                    sums[s] = jnp.where(mine, jnp.take_along_axis(block, lane, axis=1), sums[s])
        for s in range(6):
            gathered_ref[s : s + 1, here] = jnp.sum(sums[s], axis=0, keepdims=True)

    values = gathered_ref[...]
    which = lax.broadcasted_iota(jnp.int32, values.shape, 0)
    values = jnp.where(which == NVAR, slot_ref[...].astype(F32), jnp.where(which < NVAR, values, 0.0))
    high = values.astype(BF16).astype(F32)
    low = values - high

    regions = parcel_ref.shape[0]
    dest = region_ref[...]
    half = regions // 2

    for part in range(2):
        pieces = []
        for piece in (high, low):
            for d in range(half):
                pieces.append(jnp.where(dest == part * half + d, piece, 0.0))
        left = jnp.concatenate(pieces, axis=0).astype(BF16)
        placed = lax.dot_general(left, rank_hot_ref[...], (((1,), (1,)), ((), ())), preferred_element_type=F32)
        placed = placed[: half * 8] + placed[half * 8 :]
        for d in range(half):
            parcel_ref[part * half + d] = placed[d * 8 : (d + 1) * 8]
    adj_out.wait()
    metric_out.wait()


def rank_kernel(region_ref, hot_ref, rank_ref):
    entries = region_ref.shape[1]
    regions = 32
    upper = (
        lax.broadcasted_iota(jnp.int32, (LANES, LANES), 0) <= lax.broadcasted_iota(jnp.int32, (LANES, LANES), 1)
    )
    upper = jnp.where(upper, 1.0, 0.0).astype(BF16)
    region_id = lax.broadcasted_iota(jnp.int32, (regions, LANES), 0)
    carry = jnp.zeros((regions, 1), F32)
    for g in range(entries // LANES):
        here = region_id == region_ref[:, g * LANES : (g + 1) * LANES]
        hot = jnp.where(here, 1.0, 0.0)
        count = lax.dot_general(hot.astype(BF16), upper, (((1,), (0,)), ((), ())), preferred_element_type=F32) + carry
        rank_ref[:, g * LANES : (g + 1) * LANES] = jnp.sum(
            jnp.where(here, count - 1.0, 0.0), axis=0, keepdims=True
        )
        carry = count[:, LANES - 1 :]
    rank = rank_ref[...].astype(jnp.int32)
    places = lax.broadcasted_iota(jnp.int32, (CAP, entries), 0)
    hot_ref[...] = jnp.where(places == rank, 1.0, 0.0).astype(BF16)


def owner_kernel(parcel_ref, owned_ref):
    regions = parcel_ref.shape[0]
    highs = OWNED // LANES
    row_high = lax.broadcasted_iota(jnp.int32, (highs * 8, LANES), 0) // 8
    low_id = lax.broadcasted_iota(jnp.int32, (LANES, LANES), 0)
    total = jnp.zeros((2 * highs * 8, LANES), F32)
    for r in range(0, regions, 2):
        lefts, rights = [], []
        for q in (r, r + 1):
            block = parcel_ref[q]
            slot = block[NVAR : NVAR + 1, :].astype(jnp.int32)
            high = block.astype(BF16).astype(F32)
            low = block - high
            mask = row_high == slot // LANES
            tall_h = jnp.where(mask, jnp.concatenate([high] * highs, axis=0), 0.0)
            tall_l = jnp.where(mask, jnp.concatenate([low] * highs, axis=0), 0.0)
            lefts.append(jnp.concatenate([tall_h, tall_l], axis=0).astype(BF16))
            rights.append(jnp.where(low_id == slot % LANES, 1.0, 0.0).astype(BF16))
        left = jnp.concatenate(lefts, axis=1)
        right = jnp.concatenate(rights, axis=1)
        total += lax.dot_general(left, right, (((1,), (1,)), ((), ())), preferred_element_type=F32)
    total = total[: highs * 8] + total[highs * 8 :]
    for h in range(highs):
        owned_ref[:, h * LANES : (h + 1) * LANES] = total[h * 8 : h * 8 + NVAR]


def pairings():
    def swap(axis, first):
        length = lax.axis_size(axis)
        return axis, [p for i in range(first, length - 1, 2) for p in ((i, i + 1), (i + 1, i))]

    return {"ra": swap("region", 0), "rb": swap("region", 1), "sa": swap("sub", 0), "sb": swap("sub", 1)}


def exchange(sent, order):
    pairs = pairings()
    return [lax.ppermute(sent, *pairs[name]) for name in order]


def per_device(
    rhs, diag_inv, coupling, neighbours, send_tiles, tile_count, hessian, shared_vertex, owner_region, owner_slot
):
    tiles, block, width = rhs.shape
    sends = send_tiles.shape[1]
    entries = shared_vertex.shape[0]
    regions = lax.axis_size("region")
    params = pltpu.CompilerParams(vmem_limit_bytes=40 * 2**20)
    rhs = pltpu.with_memory_space_constraint(rhs, pltpu.HBM)
    diag_inv = pltpu.with_memory_space_constraint(diag_inv, pltpu.HBM)
    coupling = pltpu.with_memory_space_constraint(coupling, pltpu.HBM)
    neighbours = pltpu.with_memory_space_constraint(neighbours.T, pltpu.HBM)
    send_tiles = pltpu.with_memory_space_constraint(send_tiles, pltpu.HBM)
    vertex = shared_vertex.reshape(1, entries)
    dest = owner_region.reshape(1, entries)
    slot = owner_slot.reshape(1, entries)

    chunks = width // LANES
    adj_shape = jax.ShapeDtypeStruct((chunks, tiles * 8, LANES), F32)
    sent_shape = jax.ShapeDtypeStruct((chunks, sends * NVAR, LANES), F32)
    ext_shape = jax.ShapeDtypeStruct((chunks, tiles * 8 + 4 * sends * NVAR, LANES), F32)
    resid = pltpu.VMEM((chunks, 8, LANES), F32)
    hbm = pl.BlockSpec(memory_space=pltpu.HBM)
    smem = pl.BlockSpec(memory_space=pltpu.SMEM)
    scalars = functools.partial(pltpu.with_memory_space_constraint, memory_space=pltpu.SMEM)
    beside = pl.CostEstimate(flops=0, bytes_accessed=4 * 2**20, transcendentals=0)

    lead, sent, rhs, diag_inv, send_tiles, neighbours, listed = pl.pallas_call(
        first_kernel,
        out_shape=(
            adj_shape,
            sent_shape,
            jax.ShapeDtypeStruct(rhs.shape, rhs.dtype),
            jax.ShapeDtypeStruct(diag_inv.shape, diag_inv.dtype),
            pltpu.SMEM(send_tiles.shape, jnp.int32),
            pltpu.SMEM(neighbours.shape, jnp.int32),
            pltpu.SMEM((1, tiles), jnp.int32),
        ),
        in_specs=[hbm, hbm, smem, hbm, hbm],
        out_specs=(VMEM,) * 4 + (smem,) * 3,
        scratch_shapes=[pltpu.SemaphoreType.DMA((3,)), pltpu.SemaphoreType.DMA((2,))],
        compiler_params=params,
        name="first",
    )(send_tiles, neighbours, tile_count, rhs, diag_inv)
    send_tiles, neighbours, listed = scalars(send_tiles), scalars(neighbours), scalars(listed)
    halos = exchange(sent, ORDER)
    adjoint, coupling = pl.pallas_call(
        first_rest_kernel,
        out_shape=(adj_shape, jax.ShapeDtypeStruct(coupling.shape, coupling.dtype)),
        in_specs=[smem, smem, VMEM, VMEM, VMEM, hbm],
        out_specs=(VMEM, VMEM),
        scratch_shapes=[pltpu.SemaphoreType.DMA((4,))],
        compiler_params=params,
        cost_estimate=pl.CostEstimate(flops=0, bytes_accessed=4 * coupling.size, transcendentals=0),
        name="first_rest",
    )(listed, tile_count, rhs, diag_inv, lead, coupling)
    rank_hot = pl.pallas_call(
        rank_kernel,
        out_shape=jax.ShapeDtypeStruct((CAP, entries), BF16),
        in_specs=[VMEM],
        out_specs=VMEM,
        scratch_shapes=[pltpu.VMEM((1, entries), F32)],
        compiler_params=params,
        name="rank",
    )(dest)
    for sweep in range(SWEEPS - 1):
        order = LAST_ORDER if sweep == SWEEPS - 2 else ORDER
        lead, sent, extended = pl.pallas_call(
            functools.partial(lead_kernel, ORDER),
            out_shape=(adj_shape, sent_shape, ext_shape),
            in_specs=[smem] * 3 + [VMEM] * 8,
            out_specs=(VMEM,) * 3,
            scratch_shapes=[resid],
            compiler_params=params,
            name="lead",
        )(neighbours, send_tiles, tile_count, rhs, diag_inv, coupling, adjoint, *halos)
        halos = exchange(sent, order)
        adjoint = pl.pallas_call(
            rest_kernel,
            out_shape=adj_shape,
            in_specs=[smem] * 3 + [VMEM] * 5,
            out_specs=VMEM,
            scratch_shapes=[resid],
            compiler_params=params,
            cost_estimate=beside,
            name="rest",
        )(neighbours, listed, tile_count, rhs, diag_inv, coupling, extended, lead)
    out, metric, parcels = pl.pallas_call(
        functools.partial(last_kernel, LAST_ORDER),
        out_shape=(
            jax.ShapeDtypeStruct((tiles * 8, width), F32),
            jax.ShapeDtypeStruct((6, tiles, width), F32),
            jax.ShapeDtypeStruct((regions, 8, CAP), F32),
        ),
        in_specs=[smem, smem] + [VMEM] * 13,
        out_specs=(hbm, hbm, VMEM),
        scratch_shapes=[
            pltpu.VMEM(ext_shape.shape, F32),
            resid,
            pltpu.VMEM((tiles * 8, width), F32),
            pltpu.VMEM((6, tiles, width), F32),
            pltpu.VMEM((chunks, tiles * 8, LANES), F32),
            pltpu.VMEM((8, entries), F32),
            pltpu.SemaphoreType.DMA((2,)),
        ],
        compiler_params=params,
        name="last",
    )(
        neighbours, tile_count, rhs, diag_inv, coupling, hessian.transpose(1, 2, 0, 3), adjoint, *halos,
        vertex, dest, slot, rank_hot,
    )
    out = out.reshape(tiles, block, width)
    metric = metric.transpose(1, 0, 2)
    parcels = lax.all_to_all(parcels, "region", 0, 0, tiled=True)
    owned = pl.pallas_call(
        owner_kernel,
        out_shape=jax.ShapeDtypeStruct((6, OWNED), F32),
        in_specs=[VMEM],
        out_specs=VMEM,
        compiler_params=params,
        name="owner",
    )(parcels)
    return out, metric, owned


def solution(mesh):
    both = ("region", "sub")
    placed = (
        P(both, None, None),
        P(both, None, None, None),
        P(both, None, None, None, None),
        P(both, None),
        P(both, None),
        P(both),
        P(both, None, None, None),
        P(both),
        P(both, None),
        P(both),
    )
    return jax.shard_map(
        per_device,
        mesh=mesh,
        in_specs=placed,
        out_specs=(P(both, None, None), P(both, None, None), P(None, both)),
        check_vma=False,
    )
```

```python
import functools

import jax
import jax.numpy as jnp
from jax import lax
from jax.experimental import pallas as pl
from jax.experimental.pallas import tpu as pltpu
from jax.sharding import PartitionSpec as P

NVAR = 6
SWEEPS = 3
OWNED = 1024
CAP = 128
LANES = 128

ORDER = ("sa", "rb", "ra", "sb")
LAST_ORDER = ("ra", "sb", "sa", "rb")

F32 = jnp.float32
BF16 = jnp.bfloat16

VMEM = pl.BlockSpec(memory_space=pltpu.VMEM)


def lanes_of(q):
    return slice(q * LANES, (q + 1) * LANES)


def rows_of(t):
    return pl.ds(pl.multiple_of(t * 8, 8), 8)


def solve_tile(t, row_of, inv_ref, live):
    keep = (lax.broadcasted_iota(jnp.int32, (8, LANES), 0) < NVAR) & live
    blocks = []
    for q in range(inv_ref.shape[3] // LANES):
        total = None
        for j in range(inv_ref.shape[1]):
            term = inv_ref[t, j, :, lanes_of(q)].astype(F32) * row_of(q, j)
            total = term if total is None else total + term
        blocks.append(jnp.where(keep, total, 0.0))
    return blocks


def pack_sent(adj_ref, send_ref, sent_ref):
    for s in range(send_ref.shape[1]):
        here = rows_of(send_ref[0, s])
        for q in range(adj_ref.shape[0]):
            sent_ref[q, NVAR * s : NVAR * (s + 1), :] = adj_ref[q, here, :][:NVAR]


def fetch(pairs, sems):
    copies = [pltpu.make_async_copy(src, dst, sems.at[i]) for i, (src, dst) in enumerate(pairs)]
    for copy in copies:
        copy.start()
    return copies


def put_rows(adj_ref, t, blocks):
    for q, block in enumerate(blocks):
        adj_ref[q, rows_of(t), :] = block


def first_kernel(
    send_hbm, near_hbm, count_ref, rhs_hbm, inv_hbm,
    adj_ref, sent_ref, rhs_ref, inv_ref, send_ref, near_ref, listed_ref, sems, table_sems,
):
    send_copy, near_copy = fetch(((send_hbm, send_ref), (near_hbm, near_ref)), table_sems)
    tiles, sends = rhs_ref.shape[0], send_ref.shape[1]
    half = tiles // 2
    pairs = [(rhs_hbm, rhs_ref)]
    pairs += [(inv_hbm.at[pl.ds(p * half, half)], inv_ref.at[pl.ds(p * half, half)]) for p in range(2)]
    copies = fetch(pairs, sems)
    send_copy.wait()
    for t in range(tiles):
        listed_ref[0, t] = 0
    for s in range(sends):
        listed_ref[0, send_ref[0, s]] = 1
    for copy in copies:
        copy.wait()

    @pl.loop(0, sends)
    def _(s):
        t = send_ref[0, s]
        row_of = lambda q, j: rhs_ref[t, j : j + 1, lanes_of(q)]
        put_rows(adj_ref, t, solve_tile(t, row_of, inv_ref, t < count_ref[0]))

    pack_sent(adj_ref, send_ref, sent_ref)
    near_copy.wait()


def first_rest_kernel(listed_ref, count_ref, rhs_ref, inv_ref, lead_ref, cpl_hbm, adj_ref, cpl_ref, sems):
    parts = sems.shape[0]
    step = cpl_ref.shape[0] // parts
    some = [pl.ds(p * step, step) for p in range(parts)]
    copies = fetch([(cpl_hbm.at[s], cpl_ref.at[s]) for s in some], sems)
    adj_ref[...] = lead_ref[...]

    @pl.loop(0, rhs_ref.shape[0])
    def _(t):
        @pl.when(listed_ref[0, t] == 0)
        def _():
            row_of = lambda q, j: rhs_ref[t, j : j + 1, lanes_of(q)]
            put_rows(adj_ref, t, solve_tile(t, row_of, inv_ref, t < count_ref[0]))

    for copy in copies:
        copy.wait()


def build_extended(order, old_ref, halo_refs, ext_ref):
    own = old_ref.shape[1]
    ext_ref[:, :own, :] = old_ref[...]
    odd_region = lax.axis_index("region") % 2
    odd_sub = lax.axis_index("sub") % 2
    places = {"ra": 1 - odd_region, "rb": odd_region, "sa": 3 - odd_sub, "sb": 2 + odd_sub}
    width = halo_refs[0].shape[1]
    for name, halo in zip(order, halo_refs):
        ext_ref[:, pl.ds(pl.multiple_of(own + places[name] * width, 8), width), :] = halo[...]


def sweep_tile(t, near_ref, count_ref, rhs_ref, inv_ref, cpl_ref, ext_ref, resid_ref):
    own = rhs_ref.shape[0]
    bases = []
    for k in range(cpl_ref.shape[1]):
        tile = near_ref[k, t]
        bases.append(jnp.where(tile < own, tile * 8, tile * NVAR + own * (8 - NVAR)))
    for q in range(resid_ref.shape[0]):
        sums = [rhs_ref[t, :, lanes_of(q)], None]
        for k, base in enumerate(bases):
            for m in range(NVAR):
                term = cpl_ref[t, k, m, :, lanes_of(q)].astype(F32) * ext_ref[q, pl.ds(base + m, 1), :]
                if k % 2:
                    sums[1] = term if sums[1] is None else sums[1] + term
                else:
                    sums[0] = sums[0] - term
        resid_ref[q] = sums[0] - sums[1]
    return solve_tile(t, lambda q, j: resid_ref[q, j : j + 1, :], inv_ref, t < count_ref[0])


def lead_kernel(
    order, near_ref, send_ref, count_ref, rhs_ref, inv_ref, cpl_ref, old_ref, h0, h1, h2, h3,
    adj_ref, sent_ref, ext_ref, resid_ref,
):
    build_extended(order, old_ref, (h0, h1, h2, h3), ext_ref)

    @pl.loop(0, send_ref.shape[1])
    def _(s):
        t = send_ref[0, s]
        put_rows(adj_ref, t, sweep_tile(t, near_ref, count_ref, rhs_ref, inv_ref, cpl_ref, ext_ref, resid_ref))

    pack_sent(adj_ref, send_ref, sent_ref)


def rest_kernel(
    near_ref, listed_ref, count_ref, rhs_ref, inv_ref, cpl_ref, ext_ref, lead_ref, adj_ref, resid_ref
):
    adj_ref[...] = lead_ref[...]

    @pl.loop(0, rhs_ref.shape[0])
    def _(t):
        @pl.when(listed_ref[0, t] == 0)
        def _():
            put_rows(adj_ref, t, sweep_tile(t, near_ref, count_ref, rhs_ref, inv_ref, cpl_ref, ext_ref, resid_ref))


def last_kernel(
    order, near_ref, count_ref, rhs_ref, inv_ref, cpl_ref, hess_ref, old_ref, h0, h1, h2, h3,
    vertex_ref, region_ref, slot_ref, rank_hot_ref,
    adj_hbm, metric_hbm, parcel_ref,
    ext_ref, resid_ref, adj_ref, metric_ref, column_ref, gathered_ref, out_sems,
):
    build_extended(order, old_ref, (h0, h1, h2, h3), ext_ref)
    tiles, width = rhs_ref.shape[0], rhs_ref.shape[2]
    chunks = width // LANES

    @pl.loop(0, tiles)
    def _(t):
        blocks = sweep_tile(t, near_ref, count_ref, rhs_ref, inv_ref, cpl_ref, ext_ref, resid_ref)
        for q, block in enumerate(blocks):
            adj_ref[rows_of(t), lanes_of(q)] = block
            column_ref[q, rows_of(t), :] = jnp.abs(block)

    adj_out = pltpu.make_async_copy(adj_ref, adj_hbm, out_sems.at[0])
    adj_out.start()

    for q in range(chunks):
        sums = [None] * 6
        for c in range(NVAR):
            size = column_ref[q, pl.ds(c, tiles, stride=8), :]
            for s in range(6):
                term = hess_ref[c, s, :, lanes_of(q)].astype(F32) * size
                sums[s] = term if sums[s] is None else sums[s] + term
        for s in range(6):
            metric_ref[s, :, lanes_of(q)] = sums[s]
    metric_out = pltpu.make_async_copy(metric_ref, metric_hbm, out_sems.at[1])
    metric_out.start()

    entries = vertex_ref.shape[1]
    in_tile = lax.broadcasted_iota(jnp.int32, (8, LANES), 0)

    for g in range(entries // LANES):
        here = lanes_of(g)
        vertex = vertex_ref[:, here]
        row = jnp.broadcast_to(vertex // LANES, (8, LANES))
        lane = jnp.broadcast_to(vertex % LANES, (8, LANES))
        sums = [jnp.zeros((8, LANES), F32)] * 6
        for q in range(chunks):
            for h in range(tiles // 8):
                mine = row == (in_tile + h * 8) * chunks + q
                for s in range(6):
                    block = metric_ref[s, h * 8 : (h + 1) * 8, q * LANES : (q + 1) * LANES]
                    sums[s] = jnp.where(mine, jnp.take_along_axis(block, lane, axis=1), sums[s])
        for s in range(6):
            gathered_ref[s : s + 1, here] = jnp.sum(sums[s], axis=0, keepdims=True)

    values = gathered_ref[...]
    which = lax.broadcasted_iota(jnp.int32, values.shape, 0)
    values = jnp.where(which == NVAR, slot_ref[...].astype(F32), jnp.where(which < NVAR, values, 0.0))
    high = values.astype(BF16).astype(F32)
    low = values - high

    regions = parcel_ref.shape[0]
    dest = region_ref[...]
    half = regions // 2

    for part in range(2):
        pieces = []
        for piece in (high, low):
            for d in range(half):
                pieces.append(jnp.where(dest == part * half + d, piece, 0.0))
        left = jnp.concatenate(pieces, axis=0).astype(BF16)
        placed = lax.dot_general(left, rank_hot_ref[...], (((1,), (1,)), ((), ())), preferred_element_type=F32)
        placed = placed[: half * 8] + placed[half * 8 :]
        for d in range(half):
            parcel_ref[part * half + d] = placed[d * 8 : (d + 1) * 8]
    adj_out.wait()
    metric_out.wait()


def rank_kernel(region_ref, hot_ref, rank_ref):
    entries = region_ref.shape[1]
    regions = 32
    upper = (
        lax.broadcasted_iota(jnp.int32, (LANES, LANES), 0) <= lax.broadcasted_iota(jnp.int32, (LANES, LANES), 1)
    )
    upper = jnp.where(upper, 1.0, 0.0).astype(BF16)
    region_id = lax.broadcasted_iota(jnp.int32, (regions, LANES), 0)
    carry = jnp.zeros((regions, 1), F32)
    for g in range(entries // LANES):
        here = region_id == region_ref[:, g * LANES : (g + 1) * LANES]
        hot = jnp.where(here, 1.0, 0.0)
        count = lax.dot_general(hot.astype(BF16), upper, (((1,), (0,)), ((), ())), preferred_element_type=F32) + carry
        rank_ref[:, g * LANES : (g + 1) * LANES] = jnp.sum(
            jnp.where(here, count - 1.0, 0.0), axis=0, keepdims=True
        )
        carry = count[:, LANES - 1 :]
    rank = rank_ref[...].astype(jnp.int32)
    places = lax.broadcasted_iota(jnp.int32, (CAP, entries), 0)
    hot_ref[...] = jnp.where(places == rank, 1.0, 0.0).astype(BF16)


def owner_kernel(parcel_ref, owned_ref):
    regions = parcel_ref.shape[0]
    highs = OWNED // LANES
    row_high = lax.broadcasted_iota(jnp.int32, (highs * 8, LANES), 0) // 8
    low_id = lax.broadcasted_iota(jnp.int32, (LANES, LANES), 0)
    total = jnp.zeros((2 * highs * 8, LANES), F32)
    for r in range(0, regions, 2):
        lefts, rights = [], []
        for q in (r, r + 1):
            block = parcel_ref[q]
            slot = block[NVAR : NVAR + 1, :].astype(jnp.int32)
            high = block.astype(BF16).astype(F32)
            low = block - high
            mask = row_high == slot // LANES
            tall_h = jnp.where(mask, jnp.concatenate([high] * highs, axis=0), 0.0)
            tall_l = jnp.where(mask, jnp.concatenate([low] * highs, axis=0), 0.0)
            lefts.append(jnp.concatenate([tall_h, tall_l], axis=0).astype(BF16))
            rights.append(jnp.where(low_id == slot % LANES, 1.0, 0.0).astype(BF16))
        left = jnp.concatenate(lefts, axis=1)
        right = jnp.concatenate(rights, axis=1)
        total += lax.dot_general(left, right, (((1,), (1,)), ((), ())), preferred_element_type=F32)
    total = total[: highs * 8] + total[highs * 8 :]
    for h in range(highs):
        owned_ref[:, h * LANES : (h + 1) * LANES] = total[h * 8 : h * 8 + NVAR]


def pairings():
    def swap(axis, first):
        length = lax.axis_size(axis)
        return axis, [p for i in range(first, length - 1, 2) for p in ((i, i + 1), (i + 1, i))]

    return {"ra": swap("region", 0), "rb": swap("region", 1), "sa": swap("sub", 0), "sb": swap("sub", 1)}


def exchange(sent, order):
    pairs = pairings()
    return [lax.ppermute(sent, *pairs[name]) for name in order]


def per_device(
    rhs, diag_inv, coupling, neighbours, send_tiles, tile_count, hessian, shared_vertex, owner_region, owner_slot
):
    tiles, block, width = rhs.shape
    sends = send_tiles.shape[1]
    entries = shared_vertex.shape[0]
    regions = lax.axis_size("region")
    params = pltpu.CompilerParams(vmem_limit_bytes=40 * 2**20)
    rhs = pltpu.with_memory_space_constraint(rhs, pltpu.HBM)
    diag_inv = pltpu.with_memory_space_constraint(diag_inv, pltpu.HBM)
    coupling = pltpu.with_memory_space_constraint(coupling, pltpu.HBM)
    neighbours = pltpu.with_memory_space_constraint(neighbours.T, pltpu.HBM)
    send_tiles = pltpu.with_memory_space_constraint(send_tiles, pltpu.HBM)
    vertex = shared_vertex.reshape(1, entries)
    dest = owner_region.reshape(1, entries)
    slot = owner_slot.reshape(1, entries)

    chunks = width // LANES
    adj_shape = jax.ShapeDtypeStruct((chunks, tiles * 8, LANES), F32)
    sent_shape = jax.ShapeDtypeStruct((chunks, sends * NVAR, LANES), F32)
    ext_shape = jax.ShapeDtypeStruct((chunks, tiles * 8 + 4 * sends * NVAR, LANES), F32)
    resid = pltpu.VMEM((chunks, 8, LANES), F32)
    hbm = pl.BlockSpec(memory_space=pltpu.HBM)
    smem = pl.BlockSpec(memory_space=pltpu.SMEM)
    scalars = functools.partial(pltpu.with_memory_space_constraint, memory_space=pltpu.SMEM)
    beside = pl.CostEstimate(flops=0, bytes_accessed=4 * 2**20, transcendentals=0)

    lead, sent, rhs, diag_inv, send_tiles, neighbours, listed = pl.pallas_call(
        first_kernel,
        out_shape=(
            adj_shape,
            sent_shape,
            jax.ShapeDtypeStruct(rhs.shape, rhs.dtype),
            jax.ShapeDtypeStruct(diag_inv.shape, diag_inv.dtype),
            pltpu.SMEM(send_tiles.shape, jnp.int32),
            pltpu.SMEM(neighbours.shape, jnp.int32),
            pltpu.SMEM((1, tiles), jnp.int32),
        ),
        in_specs=[hbm, hbm, smem, hbm, hbm],
        out_specs=(VMEM,) * 4 + (smem,) * 3,
        scratch_shapes=[pltpu.SemaphoreType.DMA((3,)), pltpu.SemaphoreType.DMA((2,))],
        compiler_params=params,
        name="first",
    )(send_tiles, neighbours, tile_count, rhs, diag_inv)
    send_tiles, neighbours, listed = scalars(send_tiles), scalars(neighbours), scalars(listed)
    halos = exchange(sent, ORDER)
    adjoint, coupling = pl.pallas_call(
        first_rest_kernel,
        out_shape=(adj_shape, jax.ShapeDtypeStruct(coupling.shape, coupling.dtype)),
        in_specs=[smem, smem, VMEM, VMEM, VMEM, hbm],
        out_specs=(VMEM, VMEM),
        scratch_shapes=[pltpu.SemaphoreType.DMA((4,))],
        compiler_params=params,
        cost_estimate=pl.CostEstimate(flops=0, bytes_accessed=4 * coupling.size, transcendentals=0),
        name="first_rest",
    )(listed, tile_count, rhs, diag_inv, lead, coupling)
    rank_hot = pl.pallas_call(
        rank_kernel,
        out_shape=jax.ShapeDtypeStruct((CAP, entries), BF16),
        in_specs=[VMEM],
        out_specs=VMEM,
        scratch_shapes=[pltpu.VMEM((1, entries), F32)],
        compiler_params=params,
        name="rank",
    )(dest)
    for sweep in range(SWEEPS - 1):
        order = LAST_ORDER if sweep == SWEEPS - 2 else ORDER
        lead, sent, extended = pl.pallas_call(
            functools.partial(lead_kernel, ORDER),
            out_shape=(adj_shape, sent_shape, ext_shape),
            in_specs=[smem] * 3 + [VMEM] * 8,
            out_specs=(VMEM,) * 3,
            scratch_shapes=[resid],
            compiler_params=params,
            name="lead",
        )(neighbours, send_tiles, tile_count, rhs, diag_inv, coupling, adjoint, *halos)
        halos = exchange(sent, order)
        adjoint = pl.pallas_call(
            rest_kernel,
            out_shape=adj_shape,
            in_specs=[smem] * 3 + [VMEM] * 5,
            out_specs=VMEM,
            scratch_shapes=[resid],
            compiler_params=params,
            cost_estimate=beside,
            name="rest",
        )(neighbours, listed, tile_count, rhs, diag_inv, coupling, extended, lead)
    out, metric, parcels = pl.pallas_call(
        functools.partial(last_kernel, LAST_ORDER),
        out_shape=(
            jax.ShapeDtypeStruct((tiles * 8, width), F32),
            jax.ShapeDtypeStruct((6, tiles, width), F32),
            jax.ShapeDtypeStruct((regions, 8, CAP), F32),
        ),
        in_specs=[smem, smem] + [VMEM] * 13,
        out_specs=(hbm, hbm, VMEM),
        scratch_shapes=[
            pltpu.VMEM(ext_shape.shape, F32),
            resid,
            pltpu.VMEM((tiles * 8, width), F32),
            pltpu.VMEM((6, tiles, width), F32),
            pltpu.VMEM((chunks, tiles * 8, LANES), F32),
            pltpu.VMEM((8, entries), F32),
            pltpu.SemaphoreType.DMA((2,)),
        ],
        compiler_params=params,
        name="last",
    )(
        neighbours, tile_count, rhs, diag_inv, coupling, hessian.transpose(1, 2, 0, 3), adjoint, *halos,
        vertex, dest, slot, rank_hot,
    )
    out = out.reshape(tiles, block, width)
    metric = metric.transpose(1, 0, 2)
    parcels = lax.all_to_all(parcels, "region", 0, 0, tiled=True)
    owned = pl.pallas_call(
        owner_kernel,
        out_shape=jax.ShapeDtypeStruct((6, OWNED), F32),
        in_specs=[VMEM],
        out_specs=VMEM,
        compiler_params=params,
        name="owner",
    )(parcels)
    return out, metric, owned


def solution(mesh):
    both = ("region", "sub")
    placed = (
        P(both, None, None),
        P(both, None, None, None),
        P(both, None, None, None, None),
        P(both, None),
        P(both, None),
        P(both),
        P(both, None, None, None),
        P(both),
        P(both, None),
        P(both),
    )
    return jax.shard_map(
        per_device,
        mesh=mesh,
        in_specs=placed,
        out_specs=(P(both, None, None), P(both, None, None), P(None, both)),
        check_vma=False,
    )
```

```python
import functools

import jax
import jax.numpy as jnp
from jax import lax
from jax.experimental import pallas as pl
from jax.experimental.pallas import tpu as pltpu
from jax.sharding import PartitionSpec as P

NVAR = 6
SWEEPS = 3
OWNED = 1024
CAP = 128
LANES = 128

ORDER = ("rb", "ra", "sb", "sa")
LAST_ORDER = ("sb", "sa", "rb", "ra")

F32 = jnp.float32
BF16 = jnp.bfloat16

VMEM = pl.BlockSpec(memory_space=pltpu.VMEM)


def lanes_of(q):
    return slice(q * LANES, (q + 1) * LANES)


def rows_of(t):
    return pl.ds(pl.multiple_of(t * 8, 8), 8)


def solve_tile(t, row_of, inv_ref, live):
    keep = (lax.broadcasted_iota(jnp.int32, (8, LANES), 0) < NVAR) & live
    blocks = []
    for q in range(inv_ref.shape[3] // LANES):
        total = None
        for j in range(inv_ref.shape[1]):
            term = inv_ref[t, j, :, lanes_of(q)].astype(F32) * row_of(q, j)
            total = term if total is None else total + term
        blocks.append(jnp.where(keep, total, 0.0))
    return blocks


def pack_sent(adj_ref, send_ref, sent_ref):
    for s in range(send_ref.shape[1]):
        here = rows_of(send_ref[0, s])
        for q in range(adj_ref.shape[0]):
            sent_ref[q, NVAR * s : NVAR * (s + 1), :] = adj_ref[q, here, :][:NVAR]


def fetch(pairs, sems):
    copies = [pltpu.make_async_copy(src, dst, sems.at[i]) for i, (src, dst) in enumerate(pairs)]
    for copy in copies:
        copy.start()
    return copies


def put_rows(adj_ref, t, blocks):
    for q, block in enumerate(blocks):
        adj_ref[q, rows_of(t), :] = block


def first_kernel(
    send_hbm, near_hbm, count_ref, rhs_hbm, inv_hbm,
    adj_ref, sent_ref, rhs_ref, inv_ref, send_ref, near_ref, listed_ref, sems, table_sems,
):
    send_copy, near_copy = fetch(((send_hbm, send_ref), (near_hbm, near_ref)), table_sems)
    tiles, sends = rhs_ref.shape[0], send_ref.shape[1]
    half = tiles // 2
    pairs = [(rhs_hbm, rhs_ref)]
    pairs += [(inv_hbm.at[pl.ds(p * half, half)], inv_ref.at[pl.ds(p * half, half)]) for p in range(2)]
    copies = fetch(pairs, sems)
    send_copy.wait()
    for t in range(tiles):
        listed_ref[0, t] = 0
    for s in range(sends):
        listed_ref[0, send_ref[0, s]] = 1
    for copy in copies:
        copy.wait()

    @pl.loop(0, sends)
    def _(s):
        t = send_ref[0, s]
        row_of = lambda q, j: rhs_ref[t, j : j + 1, lanes_of(q)]
        put_rows(adj_ref, t, solve_tile(t, row_of, inv_ref, t < count_ref[0]))

    pack_sent(adj_ref, send_ref, sent_ref)
    near_copy.wait()


def first_rest_kernel(listed_ref, count_ref, rhs_ref, inv_ref, lead_ref, cpl_hbm, adj_ref, cpl_ref, sems):
    parts = sems.shape[0]
    step = cpl_ref.shape[0] // parts
    some = [pl.ds(p * step, step) for p in range(parts)]
    copies = fetch([(cpl_hbm.at[s], cpl_ref.at[s]) for s in some], sems)
    adj_ref[...] = lead_ref[...]

    @pl.loop(0, rhs_ref.shape[0])
    def _(t):
        @pl.when(listed_ref[0, t] == 0)
        def _():
            row_of = lambda q, j: rhs_ref[t, j : j + 1, lanes_of(q)]
            put_rows(adj_ref, t, solve_tile(t, row_of, inv_ref, t < count_ref[0]))

    for copy in copies:
        copy.wait()


def build_extended(order, old_ref, halo_refs, ext_ref):
    own = old_ref.shape[1]
    ext_ref[:, :own, :] = old_ref[...]
    odd_region = lax.axis_index("region") % 2
    odd_sub = lax.axis_index("sub") % 2
    places = {"ra": 1 - odd_region, "rb": odd_region, "sa": 3 - odd_sub, "sb": 2 + odd_sub}
    width = halo_refs[0].shape[1]
    for name, halo in zip(order, halo_refs):
        ext_ref[:, pl.ds(pl.multiple_of(own + places[name] * width, 8), width), :] = halo[...]


def sweep_tile(t, near_ref, count_ref, rhs_ref, inv_ref, cpl_ref, ext_ref, resid_ref):
    own = rhs_ref.shape[0]
    bases = []
    for k in range(cpl_ref.shape[1]):
        tile = near_ref[k, t]
        bases.append(jnp.where(tile < own, tile * 8, tile * NVAR + own * (8 - NVAR)))
    for q in range(resid_ref.shape[0]):
        sums = [rhs_ref[t, :, lanes_of(q)], None]
        for k, base in enumerate(bases):
            for m in range(NVAR):
                term = cpl_ref[t, k, m, :, lanes_of(q)].astype(F32) * ext_ref[q, pl.ds(base + m, 1), :]
                if k % 2:
                    sums[1] = term if sums[1] is None else sums[1] + term
                else:
                    sums[0] = sums[0] - term
        resid_ref[q] = sums[0] - sums[1]
    return solve_tile(t, lambda q, j: resid_ref[q, j : j + 1, :], inv_ref, t < count_ref[0])


def lead_kernel(
    order, near_ref, send_ref, count_ref, rhs_ref, inv_ref, cpl_ref, old_ref, h0, h1, h2, h3,
    adj_ref, sent_ref, ext_ref, resid_ref,
):
    build_extended(order, old_ref, (h0, h1, h2, h3), ext_ref)

    @pl.loop(0, send_ref.shape[1])
    def _(s):
        t = send_ref[0, s]
        put_rows(adj_ref, t, sweep_tile(t, near_ref, count_ref, rhs_ref, inv_ref, cpl_ref, ext_ref, resid_ref))

    pack_sent(adj_ref, send_ref, sent_ref)


def rest_kernel(
    near_ref, listed_ref, count_ref, rhs_ref, inv_ref, cpl_ref, ext_ref, lead_ref, adj_ref, resid_ref
):
    adj_ref[...] = lead_ref[...]

    @pl.loop(0, rhs_ref.shape[0])
    def _(t):
        @pl.when(listed_ref[0, t] == 0)
        def _():
            put_rows(adj_ref, t, sweep_tile(t, near_ref, count_ref, rhs_ref, inv_ref, cpl_ref, ext_ref, resid_ref))


def last_kernel(
    order, near_ref, count_ref, rhs_ref, inv_ref, cpl_ref, hess_ref, old_ref, h0, h1, h2, h3,
    vertex_ref, region_ref, slot_ref, rank_hot_ref,
    adj_hbm, metric_hbm, parcel_ref,
    ext_ref, resid_ref, adj_ref, metric_ref, column_ref, gathered_ref, out_sems,
):
    build_extended(order, old_ref, (h0, h1, h2, h3), ext_ref)
    tiles, width = rhs_ref.shape[0], rhs_ref.shape[2]
    chunks = width // LANES

    @pl.loop(0, tiles)
    def _(t):
        blocks = sweep_tile(t, near_ref, count_ref, rhs_ref, inv_ref, cpl_ref, ext_ref, resid_ref)
        for q, block in enumerate(blocks):
            adj_ref[rows_of(t), lanes_of(q)] = block
            column_ref[q, rows_of(t), :] = jnp.abs(block)

    adj_out = pltpu.make_async_copy(adj_ref, adj_hbm, out_sems.at[0])
    adj_out.start()

    for q in range(chunks):
        sums = [None] * 6
        for c in range(NVAR):
            size = column_ref[q, pl.ds(c, tiles, stride=8), :]
            for s in range(6):
                term = hess_ref[c, s, :, lanes_of(q)].astype(F32) * size
                sums[s] = term if sums[s] is None else sums[s] + term
        for s in range(6):
            metric_ref[s, :, lanes_of(q)] = sums[s]
    metric_out = pltpu.make_async_copy(metric_ref, metric_hbm, out_sems.at[1])
    metric_out.start()

    entries = vertex_ref.shape[1]
    in_tile = lax.broadcasted_iota(jnp.int32, (8, LANES), 0)

    for g in range(entries // LANES):
        here = lanes_of(g)
        vertex = vertex_ref[:, here]
        row = jnp.broadcast_to(vertex // LANES, (8, LANES))
        lane = jnp.broadcast_to(vertex % LANES, (8, LANES))
        sums = [jnp.zeros((8, LANES), F32)] * 6
        for q in range(chunks):
            for h in range(tiles // 8):
                mine = row == (in_tile + h * 8) * chunks + q
                for s in range(6):
                    block = metric_ref[s, h * 8 : (h + 1) * 8, q * LANES : (q + 1) * LANES]
                    sums[s] = jnp.where(mine, jnp.take_along_axis(block, lane, axis=1), sums[s])
        for s in range(6):
            gathered_ref[s : s + 1, here] = jnp.sum(sums[s], axis=0, keepdims=True)

    values = gathered_ref[...]
    which = lax.broadcasted_iota(jnp.int32, values.shape, 0)
    values = jnp.where(which == NVAR, slot_ref[...].astype(F32), jnp.where(which < NVAR, values, 0.0))
    high = values.astype(BF16).astype(F32)
    low = values - high

    regions = parcel_ref.shape[0]
    dest = region_ref[...]
    half = regions // 2

    for part in range(2):
        pieces = []
        for piece in (high, low):
            for d in range(half):
                pieces.append(jnp.where(dest == part * half + d, piece, 0.0))
        left = jnp.concatenate(pieces, axis=0).astype(BF16)
        placed = lax.dot_general(left, rank_hot_ref[...], (((1,), (1,)), ((), ())), preferred_element_type=F32)
        placed = placed[: half * 8] + placed[half * 8 :]
        for d in range(half):
            parcel_ref[part * half + d] = placed[d * 8 : (d + 1) * 8]
    adj_out.wait()
    metric_out.wait()


def rank_kernel(region_ref, hot_ref, rank_ref):
    entries = region_ref.shape[1]
    regions = 32
    upper = (
        lax.broadcasted_iota(jnp.int32, (LANES, LANES), 0) <= lax.broadcasted_iota(jnp.int32, (LANES, LANES), 1)
    )
    upper = jnp.where(upper, 1.0, 0.0).astype(BF16)
    region_id = lax.broadcasted_iota(jnp.int32, (regions, LANES), 0)
    carry = jnp.zeros((regions, 1), F32)
    for g in range(entries // LANES):
        here = region_id == region_ref[:, g * LANES : (g + 1) * LANES]
        hot = jnp.where(here, 1.0, 0.0)
        count = lax.dot_general(hot.astype(BF16), upper, (((1,), (0,)), ((), ())), preferred_element_type=F32) + carry
        rank_ref[:, g * LANES : (g + 1) * LANES] = jnp.sum(
            jnp.where(here, count - 1.0, 0.0), axis=0, keepdims=True
        )
        carry = count[:, LANES - 1 :]
    rank = rank_ref[...].astype(jnp.int32)
    places = lax.broadcasted_iota(jnp.int32, (CAP, entries), 0)
    hot_ref[...] = jnp.where(places == rank, 1.0, 0.0).astype(BF16)


def owner_kernel(parcel_ref, owned_ref):
    regions = parcel_ref.shape[0]
    highs = OWNED // LANES
    row_high = lax.broadcasted_iota(jnp.int32, (highs * 8, LANES), 0) // 8
    low_id = lax.broadcasted_iota(jnp.int32, (LANES, LANES), 0)
    total = jnp.zeros((2 * highs * 8, LANES), F32)
    for r in range(0, regions, 2):
        lefts, rights = [], []
        for q in (r, r + 1):
            block = parcel_ref[q]
            slot = block[NVAR : NVAR + 1, :].astype(jnp.int32)
            high = block.astype(BF16).astype(F32)
            low = block - high
            mask = row_high == slot // LANES
            tall_h = jnp.where(mask, jnp.concatenate([high] * highs, axis=0), 0.0)
            tall_l = jnp.where(mask, jnp.concatenate([low] * highs, axis=0), 0.0)
            lefts.append(jnp.concatenate([tall_h, tall_l], axis=0).astype(BF16))
            rights.append(jnp.where(low_id == slot % LANES, 1.0, 0.0).astype(BF16))
        left = jnp.concatenate(lefts, axis=1)
        right = jnp.concatenate(rights, axis=1)
        total += lax.dot_general(left, right, (((1,), (1,)), ((), ())), preferred_element_type=F32)
    total = total[: highs * 8] + total[highs * 8 :]
    for h in range(highs):
        owned_ref[:, h * LANES : (h + 1) * LANES] = total[h * 8 : h * 8 + NVAR]


def pairings():
    def swap(axis, first):
        length = lax.axis_size(axis)
        return axis, [p for i in range(first, length - 1, 2) for p in ((i, i + 1), (i + 1, i))]

    return {"ra": swap("region", 0), "rb": swap("region", 1), "sa": swap("sub", 0), "sb": swap("sub", 1)}


def exchange(sent, order):
    pairs = pairings()
    return [lax.ppermute(sent, *pairs[name]) for name in order]


def per_device(
    rhs, diag_inv, coupling, neighbours, send_tiles, tile_count, hessian, shared_vertex, owner_region, owner_slot
):
    tiles, block, width = rhs.shape
    sends = send_tiles.shape[1]
    entries = shared_vertex.shape[0]
    regions = lax.axis_size("region")
    params = pltpu.CompilerParams(vmem_limit_bytes=40 * 2**20)
    rhs = pltpu.with_memory_space_constraint(rhs, pltpu.HBM)
    diag_inv = pltpu.with_memory_space_constraint(diag_inv, pltpu.HBM)
    coupling = pltpu.with_memory_space_constraint(coupling, pltpu.HBM)
    neighbours = pltpu.with_memory_space_constraint(neighbours.T, pltpu.HBM)
    send_tiles = pltpu.with_memory_space_constraint(send_tiles, pltpu.HBM)
    vertex = shared_vertex.reshape(1, entries)
    dest = owner_region.reshape(1, entries)
    slot = owner_slot.reshape(1, entries)

    chunks = width // LANES
    adj_shape = jax.ShapeDtypeStruct((chunks, tiles * 8, LANES), F32)
    sent_shape = jax.ShapeDtypeStruct((chunks, sends * NVAR, LANES), F32)
    ext_shape = jax.ShapeDtypeStruct((chunks, tiles * 8 + 4 * sends * NVAR, LANES), F32)
    resid = pltpu.VMEM((chunks, 8, LANES), F32)
    hbm = pl.BlockSpec(memory_space=pltpu.HBM)
    smem = pl.BlockSpec(memory_space=pltpu.SMEM)
    scalars = functools.partial(pltpu.with_memory_space_constraint, memory_space=pltpu.SMEM)
    beside = pl.CostEstimate(flops=0, bytes_accessed=4 * 2**20, transcendentals=0)

    lead, sent, rhs, diag_inv, send_tiles, neighbours, listed = pl.pallas_call(
        first_kernel,
        out_shape=(
            adj_shape,
            sent_shape,
            jax.ShapeDtypeStruct(rhs.shape, rhs.dtype),
            jax.ShapeDtypeStruct(diag_inv.shape, diag_inv.dtype),
            pltpu.SMEM(send_tiles.shape, jnp.int32),
            pltpu.SMEM(neighbours.shape, jnp.int32),
            pltpu.SMEM((1, tiles), jnp.int32),
        ),
        in_specs=[hbm, hbm, smem, hbm, hbm],
        out_specs=(VMEM,) * 4 + (smem,) * 3,
        scratch_shapes=[pltpu.SemaphoreType.DMA((3,)), pltpu.SemaphoreType.DMA((2,))],
        compiler_params=params,
        name="first",
    )(send_tiles, neighbours, tile_count, rhs, diag_inv)
    send_tiles, neighbours, listed = scalars(send_tiles), scalars(neighbours), scalars(listed)
    halos = exchange(sent, ORDER)
    adjoint, coupling = pl.pallas_call(
        first_rest_kernel,
        out_shape=(adj_shape, jax.ShapeDtypeStruct(coupling.shape, coupling.dtype)),
        in_specs=[smem, smem, VMEM, VMEM, VMEM, hbm],
        out_specs=(VMEM, VMEM),
        scratch_shapes=[pltpu.SemaphoreType.DMA((4,))],
        compiler_params=params,
        cost_estimate=pl.CostEstimate(flops=0, bytes_accessed=4 * coupling.size, transcendentals=0),
        name="first_rest",
    )(listed, tile_count, rhs, diag_inv, lead, coupling)
    rank_hot = pl.pallas_call(
        rank_kernel,
        out_shape=jax.ShapeDtypeStruct((CAP, entries), BF16),
        in_specs=[VMEM],
        out_specs=VMEM,
        scratch_shapes=[pltpu.VMEM((1, entries), F32)],
        compiler_params=params,
        name="rank",
    )(dest)
    for sweep in range(SWEEPS - 1):
        order = LAST_ORDER if sweep == SWEEPS - 2 else ORDER
        lead, sent, extended = pl.pallas_call(
            functools.partial(lead_kernel, ORDER),
            out_shape=(adj_shape, sent_shape, ext_shape),
            in_specs=[smem] * 3 + [VMEM] * 8,
            out_specs=(VMEM,) * 3,
            scratch_shapes=[resid],
            compiler_params=params,
            name="lead",
        )(neighbours, send_tiles, tile_count, rhs, diag_inv, coupling, adjoint, *halos)
        halos = exchange(sent, order)
        adjoint = pl.pallas_call(
            rest_kernel,
            out_shape=adj_shape,
            in_specs=[smem] * 3 + [VMEM] * 5,
            out_specs=VMEM,
            scratch_shapes=[resid],
            compiler_params=params,
            cost_estimate=beside,
            name="rest",
        )(neighbours, listed, tile_count, rhs, diag_inv, coupling, extended, lead)
    out, metric, parcels = pl.pallas_call(
        functools.partial(last_kernel, LAST_ORDER),
        out_shape=(
            jax.ShapeDtypeStruct((tiles * 8, width), F32),
            jax.ShapeDtypeStruct((6, tiles, width), F32),
            jax.ShapeDtypeStruct((regions, 8, CAP), F32),
        ),
        in_specs=[smem, smem] + [VMEM] * 13,
        out_specs=(hbm, hbm, VMEM),
        scratch_shapes=[
            pltpu.VMEM(ext_shape.shape, F32),
            resid,
            pltpu.VMEM((tiles * 8, width), F32),
            pltpu.VMEM((6, tiles, width), F32),
            pltpu.VMEM((chunks, tiles * 8, LANES), F32),
            pltpu.VMEM((8, entries), F32),
            pltpu.SemaphoreType.DMA((2,)),
        ],
        compiler_params=params,
        name="last",
    )(
        neighbours, tile_count, rhs, diag_inv, coupling, hessian.transpose(1, 2, 0, 3), adjoint, *halos,
        vertex, dest, slot, rank_hot,
    )
    out = out.reshape(tiles, block, width)
    metric = metric.transpose(1, 0, 2)
    parcels = lax.all_to_all(parcels, "region", 0, 0, tiled=True)
    owned = pl.pallas_call(
        owner_kernel,
        out_shape=jax.ShapeDtypeStruct((6, OWNED), F32),
        in_specs=[VMEM],
        out_specs=VMEM,
        compiler_params=params,
        name="owner",
    )(parcels)
    return out, metric, owned


def solution(mesh):
    both = ("region", "sub")
    placed = (
        P(both, None, None),
        P(both, None, None, None),
        P(both, None, None, None, None),
        P(both, None),
        P(both, None),
        P(both),
        P(both, None, None, None),
        P(both),
        P(both, None),
        P(both),
    )
    return jax.shard_map(
        per_device,
        mesh=mesh,
        in_specs=placed,
        out_specs=(P(both, None, None), P(both, None, None), P(None, both)),
        check_vma=False,
    )
```

```python
import functools

import jax
import jax.numpy as jnp
from jax import lax
from jax.experimental import pallas as pl
from jax.experimental.pallas import tpu as pltpu
from jax.sharding import PartitionSpec as P

NVAR = 6
SWEEPS = 3
OWNED = 1024
CAP = 128
LANES = 128

ORDER = ("rb", "ra", "sb", "sa")
LAST_ORDER = ("sb", "sa", "rb", "ra")

F32 = jnp.float32
BF16 = jnp.bfloat16

VMEM = pl.BlockSpec(memory_space=pltpu.VMEM)


def lanes_of(q):
    return slice(q * LANES, (q + 1) * LANES)


def rows_of(t):
    return pl.ds(pl.multiple_of(t * 8, 8), 8)


def solve_tile(t, row_of, inv_ref, live):
    keep = (lax.broadcasted_iota(jnp.int32, (8, LANES), 0) < NVAR) & live
    blocks = []
    for q in range(inv_ref.shape[3] // LANES):
        total = None
        for j in range(inv_ref.shape[1]):
            term = inv_ref[t, j, :, lanes_of(q)].astype(F32) * row_of(q, j)
            total = term if total is None else total + term
        blocks.append(jnp.where(keep, total, 0.0))
    return blocks


def pack_sent(adj_ref, send_ref, sent_ref):
    for s in range(send_ref.shape[1]):
        here = rows_of(send_ref[0, s])
        for q in range(adj_ref.shape[0]):
            sent_ref[q, NVAR * s : NVAR * (s + 1), :] = adj_ref[q, here, :][:NVAR]


def fetch(pairs, sems):
    copies = [pltpu.make_async_copy(src, dst, sems.at[i]) for i, (src, dst) in enumerate(pairs)]
    for copy in copies:
        copy.start()
    return copies


def put_rows(adj_ref, t, blocks):
    for q, block in enumerate(blocks):
        adj_ref[q, rows_of(t), :] = block


def first_kernel(
    send_hbm, near_hbm, count_ref, rhs_hbm, inv_hbm,
    adj_ref, sent_ref, rhs_ref, inv_ref, send_ref, near_ref, listed_ref, sems, table_sems,
):
    send_copy, near_copy = fetch(((send_hbm, send_ref), (near_hbm, near_ref)), table_sems)
    tiles, sends = rhs_ref.shape[0], send_ref.shape[1]
    half = tiles // 2
    pairs = [(rhs_hbm, rhs_ref)]
    pairs += [(inv_hbm.at[pl.ds(p * half, half)], inv_ref.at[pl.ds(p * half, half)]) for p in range(2)]
    copies = fetch(pairs, sems)
    send_copy.wait()
    for t in range(tiles):
        listed_ref[0, t] = 0
    for s in range(sends):
        listed_ref[0, send_ref[0, s]] = 1
    for copy in copies:
        copy.wait()

    @pl.loop(0, sends)
    def _(s):
        t = send_ref[0, s]
        row_of = lambda q, j: rhs_ref[t, j : j + 1, lanes_of(q)]
        put_rows(adj_ref, t, solve_tile(t, row_of, inv_ref, t < count_ref[0]))

    pack_sent(adj_ref, send_ref, sent_ref)
    near_copy.wait()


def first_rest_kernel(listed_ref, count_ref, rhs_ref, inv_ref, lead_ref, cpl_hbm, adj_ref, cpl_ref, sems):
    parts = sems.shape[0]
    step = cpl_ref.shape[0] // parts
    some = [pl.ds(p * step, step) for p in range(parts)]
    copies = fetch([(cpl_hbm.at[s], cpl_ref.at[s]) for s in some], sems)
    adj_ref[...] = lead_ref[...]

    @pl.loop(0, rhs_ref.shape[0])
    def _(t):
        @pl.when(listed_ref[0, t] == 0)
        def _():
            row_of = lambda q, j: rhs_ref[t, j : j + 1, lanes_of(q)]
            put_rows(adj_ref, t, solve_tile(t, row_of, inv_ref, t < count_ref[0]))

    for copy in copies:
        copy.wait()


def build_extended(order, old_ref, halo_refs, ext_ref):
    own = old_ref.shape[1]
    ext_ref[:, :own, :] = old_ref[...]
    odd_region = lax.axis_index("region") % 2
    odd_sub = lax.axis_index("sub") % 2
    places = {"ra": 1 - odd_region, "rb": odd_region, "sa": 3 - odd_sub, "sb": 2 + odd_sub}
    width = halo_refs[0].shape[1]
    for name, halo in zip(order, halo_refs):
        ext_ref[:, pl.ds(pl.multiple_of(own + places[name] * width, 8), width), :] = halo[...]


def sweep_tile(t, near_ref, count_ref, rhs_ref, inv_ref, cpl_ref, ext_ref, resid_ref):
    own = rhs_ref.shape[0]
    bases = []
    for k in range(cpl_ref.shape[1]):
        tile = near_ref[k, t]
        bases.append(jnp.where(tile < own, tile * 8, tile * NVAR + own * (8 - NVAR)))
    for q in range(resid_ref.shape[0]):
        sums = [rhs_ref[t, :, lanes_of(q)], None]
        for k, base in enumerate(bases):
            for m in range(NVAR):
                term = cpl_ref[t, k, m, :, lanes_of(q)].astype(F32) * ext_ref[q, pl.ds(base + m, 1), :]
                if k % 2:
                    sums[1] = term if sums[1] is None else sums[1] + term
                else:
                    sums[0] = sums[0] - term
        resid_ref[q] = sums[0] - sums[1]
    return solve_tile(t, lambda q, j: resid_ref[q, j : j + 1, :], inv_ref, t < count_ref[0])


def lead_kernel(
    order, near_ref, send_ref, count_ref, rhs_ref, inv_ref, cpl_ref, old_ref, h0, h1, h2, h3,
    adj_ref, sent_ref, ext_ref, resid_ref,
):
    build_extended(order, old_ref, (h0, h1, h2, h3), ext_ref)

    @pl.loop(0, send_ref.shape[1])
    def _(s):
        t = send_ref[0, s]
        put_rows(adj_ref, t, sweep_tile(t, near_ref, count_ref, rhs_ref, inv_ref, cpl_ref, ext_ref, resid_ref))

    pack_sent(adj_ref, send_ref, sent_ref)


def rest_kernel(
    near_ref, listed_ref, count_ref, rhs_ref, inv_ref, cpl_ref, ext_ref, lead_ref, adj_ref, resid_ref
):
    adj_ref[...] = lead_ref[...]

    @pl.loop(0, rhs_ref.shape[0])
    def _(t):
        @pl.when(listed_ref[0, t] == 0)
        def _():
            put_rows(adj_ref, t, sweep_tile(t, near_ref, count_ref, rhs_ref, inv_ref, cpl_ref, ext_ref, resid_ref))


def last_kernel(
    order, near_ref, count_ref, rhs_ref, inv_ref, cpl_ref, hess_ref, old_ref, h0, h1, h2, h3,
    vertex_ref, region_ref, slot_ref, rank_hot_ref,
    adj_hbm, metric_hbm, parcel_ref,
    ext_ref, resid_ref, adj_ref, metric_ref, column_ref, gathered_ref, out_sems,
):
    build_extended(order, old_ref, (h0, h1, h2, h3), ext_ref)
    tiles, width = rhs_ref.shape[0], rhs_ref.shape[2]
    chunks = width // LANES

    @pl.loop(0, tiles)
    def _(t):
        blocks = sweep_tile(t, near_ref, count_ref, rhs_ref, inv_ref, cpl_ref, ext_ref, resid_ref)
        for q, block in enumerate(blocks):
            adj_ref[rows_of(t), lanes_of(q)] = block
            column_ref[q, rows_of(t), :] = jnp.abs(block)

    adj_out = pltpu.make_async_copy(adj_ref, adj_hbm, out_sems.at[0])
    adj_out.start()

    for q in range(chunks):
        sums = [None] * 6
        for c in range(NVAR):
            size = column_ref[q, pl.ds(c, tiles, stride=8), :]
            for s in range(6):
                term = hess_ref[c, s, :, lanes_of(q)].astype(F32) * size
                sums[s] = term if sums[s] is None else sums[s] + term
        for s in range(6):
            metric_ref[s, :, lanes_of(q)] = sums[s]
    metric_out = pltpu.make_async_copy(metric_ref, metric_hbm, out_sems.at[1])
    metric_out.start()

    entries = vertex_ref.shape[1]
    in_tile = lax.broadcasted_iota(jnp.int32, (8, LANES), 0)

    for g in range(entries // LANES):
        here = lanes_of(g)
        vertex = vertex_ref[:, here]
        row = jnp.broadcast_to(vertex // LANES, (8, LANES))
        lane = jnp.broadcast_to(vertex % LANES, (8, LANES))
        sums = [jnp.zeros((8, LANES), F32)] * 6
        for q in range(chunks):
            for h in range(tiles // 8):
                mine = row == (in_tile + h * 8) * chunks + q
                for s in range(6):
                    block = metric_ref[s, h * 8 : (h + 1) * 8, q * LANES : (q + 1) * LANES]
                    sums[s] = jnp.where(mine, jnp.take_along_axis(block, lane, axis=1), sums[s])
        for s in range(6):
            gathered_ref[s : s + 1, here] = jnp.sum(sums[s], axis=0, keepdims=True)

    values = gathered_ref[...]
    which = lax.broadcasted_iota(jnp.int32, values.shape, 0)
    values = jnp.where(which == NVAR, slot_ref[...].astype(F32), jnp.where(which < NVAR, values, 0.0))
    high = values.astype(BF16).astype(F32)
    low = values - high

    regions = parcel_ref.shape[0]
    dest = region_ref[...]
    half = regions // 2

    for part in range(2):
        pieces = []
        for piece in (high, low):
            for d in range(half):
                pieces.append(jnp.where(dest == part * half + d, piece, 0.0))
        left = jnp.concatenate(pieces, axis=0).astype(BF16)
        placed = lax.dot_general(left, rank_hot_ref[...], (((1,), (1,)), ((), ())), preferred_element_type=F32)
        placed = placed[: half * 8] + placed[half * 8 :]
        for d in range(half):
            parcel_ref[part * half + d] = placed[d * 8 : (d + 1) * 8]
    adj_out.wait()
    metric_out.wait()


def rank_kernel(region_ref, hot_ref, rank_ref):
    entries = region_ref.shape[1]
    regions = 32
    upper = (
        lax.broadcasted_iota(jnp.int32, (LANES, LANES), 0) <= lax.broadcasted_iota(jnp.int32, (LANES, LANES), 1)
    )
    upper = jnp.where(upper, 1.0, 0.0).astype(BF16)
    region_id = lax.broadcasted_iota(jnp.int32, (regions, LANES), 0)
    carry = jnp.zeros((regions, 1), F32)
    for g in range(entries // LANES):
        here = region_id == region_ref[:, g * LANES : (g + 1) * LANES]
        hot = jnp.where(here, 1.0, 0.0)
        count = lax.dot_general(hot.astype(BF16), upper, (((1,), (0,)), ((), ())), preferred_element_type=F32) + carry
        rank_ref[:, g * LANES : (g + 1) * LANES] = jnp.sum(
            jnp.where(here, count - 1.0, 0.0), axis=0, keepdims=True
        )
        carry = count[:, LANES - 1 :]
    rank = rank_ref[...].astype(jnp.int32)
    places = lax.broadcasted_iota(jnp.int32, (CAP, entries), 0)
    hot_ref[...] = jnp.where(places == rank, 1.0, 0.0).astype(BF16)


def owner_kernel(parcel_ref, owned_ref):
    regions = parcel_ref.shape[0]
    highs = OWNED // LANES
    row_high = lax.broadcasted_iota(jnp.int32, (highs * 8, LANES), 0) // 8
    low_id = lax.broadcasted_iota(jnp.int32, (LANES, LANES), 0)
    total = jnp.zeros((2 * highs * 8, LANES), F32)
    for r in range(0, regions, 2):
        lefts, rights = [], []
        for q in (r, r + 1):
            block = parcel_ref[q]
            slot = block[NVAR : NVAR + 1, :].astype(jnp.int32)
            high = block.astype(BF16).astype(F32)
            low = block - high
            mask = row_high == slot // LANES
            tall_h = jnp.where(mask, jnp.concatenate([high] * highs, axis=0), 0.0)
            tall_l = jnp.where(mask, jnp.concatenate([low] * highs, axis=0), 0.0)
            lefts.append(jnp.concatenate([tall_h, tall_l], axis=0).astype(BF16))
            rights.append(jnp.where(low_id == slot % LANES, 1.0, 0.0).astype(BF16))
        left = jnp.concatenate(lefts, axis=1)
        right = jnp.concatenate(rights, axis=1)
        total += lax.dot_general(left, right, (((1,), (1,)), ((), ())), preferred_element_type=F32)
    total = total[: highs * 8] + total[highs * 8 :]
    for h in range(highs):
        owned_ref[:, h * LANES : (h + 1) * LANES] = total[h * 8 : h * 8 + NVAR]


def pairings():
    def swap(axis, first):
        length = lax.axis_size(axis)
        return axis, [p for i in range(first, length - 1, 2) for p in ((i, i + 1), (i + 1, i))]

    return {"ra": swap("region", 0), "rb": swap("region", 1), "sa": swap("sub", 0), "sb": swap("sub", 1)}


def exchange(sent, order):
    pairs = pairings()
    return [lax.ppermute(sent, *pairs[name]) for name in order]


def per_device(
    rhs, diag_inv, coupling, neighbours, send_tiles, tile_count, hessian, shared_vertex, owner_region, owner_slot
):
    tiles, block, width = rhs.shape
    sends = send_tiles.shape[1]
    entries = shared_vertex.shape[0]
    regions = lax.axis_size("region")
    params = pltpu.CompilerParams(vmem_limit_bytes=40 * 2**20)
    rhs = pltpu.with_memory_space_constraint(rhs, pltpu.HBM)
    diag_inv = pltpu.with_memory_space_constraint(diag_inv, pltpu.HBM)
    coupling = pltpu.with_memory_space_constraint(coupling, pltpu.HBM)
    neighbours = pltpu.with_memory_space_constraint(neighbours.T, pltpu.HBM)
    send_tiles = pltpu.with_memory_space_constraint(send_tiles, pltpu.HBM)
    vertex = shared_vertex.reshape(1, entries)
    dest = owner_region.reshape(1, entries)
    slot = owner_slot.reshape(1, entries)

    chunks = width // LANES
    adj_shape = jax.ShapeDtypeStruct((chunks, tiles * 8, LANES), F32)
    sent_shape = jax.ShapeDtypeStruct((chunks, sends * NVAR, LANES), F32)
    ext_shape = jax.ShapeDtypeStruct((chunks, tiles * 8 + 4 * sends * NVAR, LANES), F32)
    resid = pltpu.VMEM((chunks, 8, LANES), F32)
    hbm = pl.BlockSpec(memory_space=pltpu.HBM)
    smem = pl.BlockSpec(memory_space=pltpu.SMEM)
    scalars = functools.partial(pltpu.with_memory_space_constraint, memory_space=pltpu.SMEM)
    beside = pl.CostEstimate(flops=0, bytes_accessed=4 * 2**20, transcendentals=0)

    lead, sent, rhs, diag_inv, send_tiles, neighbours, listed = pl.pallas_call(
        first_kernel,
        out_shape=(
            adj_shape,
            sent_shape,
            jax.ShapeDtypeStruct(rhs.shape, rhs.dtype),
            jax.ShapeDtypeStruct(diag_inv.shape, diag_inv.dtype),
            pltpu.SMEM(send_tiles.shape, jnp.int32),
            pltpu.SMEM(neighbours.shape, jnp.int32),
            pltpu.SMEM((1, tiles), jnp.int32),
        ),
        in_specs=[hbm, hbm, smem, hbm, hbm],
        out_specs=(VMEM,) * 4 + (smem,) * 3,
        scratch_shapes=[pltpu.SemaphoreType.DMA((3,)), pltpu.SemaphoreType.DMA((2,))],
        compiler_params=params,
        name="first",
    )(send_tiles, neighbours, tile_count, rhs, diag_inv)
    send_tiles, neighbours, listed = scalars(send_tiles), scalars(neighbours), scalars(listed)
    halos = exchange(sent, ORDER)
    adjoint, coupling = pl.pallas_call(
        first_rest_kernel,
        out_shape=(adj_shape, jax.ShapeDtypeStruct(coupling.shape, coupling.dtype)),
        in_specs=[smem, smem, VMEM, VMEM, VMEM, hbm],
        out_specs=(VMEM, VMEM),
        scratch_shapes=[pltpu.SemaphoreType.DMA((tiles,))],
        compiler_params=params,
        cost_estimate=pl.CostEstimate(flops=0, bytes_accessed=4 * coupling.size, transcendentals=0),
        name="first_rest",
    )(listed, tile_count, rhs, diag_inv, lead, coupling)
    rank_hot = pl.pallas_call(
        rank_kernel,
        out_shape=jax.ShapeDtypeStruct((CAP, entries), BF16),
        in_specs=[VMEM],
        out_specs=VMEM,
        scratch_shapes=[pltpu.VMEM((1, entries), F32)],
        compiler_params=params,
        name="rank",
    )(dest)
    for sweep in range(SWEEPS - 1):
        order = LAST_ORDER if sweep == SWEEPS - 2 else ORDER
        lead, sent, extended = pl.pallas_call(
            functools.partial(lead_kernel, ORDER),
            out_shape=(adj_shape, sent_shape, ext_shape),
            in_specs=[smem] * 3 + [VMEM] * 8,
            out_specs=(VMEM,) * 3,
            scratch_shapes=[resid],
            compiler_params=params,
            name="lead",
        )(neighbours, send_tiles, tile_count, rhs, diag_inv, coupling, adjoint, *halos)
        halos = exchange(sent, order)
        adjoint = pl.pallas_call(
            rest_kernel,
            out_shape=adj_shape,
            in_specs=[smem] * 3 + [VMEM] * 5,
            out_specs=VMEM,
            scratch_shapes=[resid],
            compiler_params=params,
            cost_estimate=beside,
            name="rest",
        )(neighbours, listed, tile_count, rhs, diag_inv, coupling, extended, lead)
    out, metric, parcels = pl.pallas_call(
        functools.partial(last_kernel, LAST_ORDER),
        out_shape=(
            jax.ShapeDtypeStruct((tiles * 8, width), F32),
            jax.ShapeDtypeStruct((6, tiles, width), F32),
            jax.ShapeDtypeStruct((regions, 8, CAP), F32),
        ),
        in_specs=[smem, smem] + [VMEM] * 13,
        out_specs=(hbm, hbm, VMEM),
        scratch_shapes=[
            pltpu.VMEM(ext_shape.shape, F32),
            resid,
            pltpu.VMEM((tiles * 8, width), F32),
            pltpu.VMEM((6, tiles, width), F32),
            pltpu.VMEM((chunks, tiles * 8, LANES), F32),
            pltpu.VMEM((8, entries), F32),
            pltpu.SemaphoreType.DMA((2,)),
        ],
        compiler_params=params,
        name="last",
    )(
        neighbours, tile_count, rhs, diag_inv, coupling, hessian.transpose(1, 2, 0, 3), adjoint, *halos,
        vertex, dest, slot, rank_hot,
    )
    out = out.reshape(tiles, block, width)
    metric = metric.transpose(1, 0, 2)
    parcels = lax.all_to_all(parcels, "region", 0, 0, tiled=True)
    owned = pl.pallas_call(
        owner_kernel,
        out_shape=jax.ShapeDtypeStruct((6, OWNED), F32),
        in_specs=[VMEM],
        out_specs=VMEM,
        compiler_params=params,
        name="owner",
    )(parcels)
    return out, metric, owned


def solution(mesh):
    both = ("region", "sub")
    placed = (
        P(both, None, None),
        P(both, None, None, None),
        P(both, None, None, None, None),
        P(both, None),
        P(both, None),
        P(both),
        P(both, None, None, None),
        P(both),
        P(both, None),
        P(both),
    )
    return jax.shard_map(
        per_device,
        mesh=mesh,
        in_specs=placed,
        out_specs=(P(both, None, None), P(both, None, None), P(None, both)),
        check_vma=False,
    )
```

```python
import functools

import jax
import jax.numpy as jnp
from jax import lax
from jax.experimental import pallas as pl
from jax.experimental.pallas import tpu as pltpu
from jax.sharding import PartitionSpec as P

NVAR = 6
SWEEPS = 3
OWNED = 1024
CAP = 128
LANES = 128

ORDER = ("rb", "ra", "sb", "sa")
LAST_ORDER = ("sb", "ra", "sa", "rb")

F32 = jnp.float32
BF16 = jnp.bfloat16

VMEM = pl.BlockSpec(memory_space=pltpu.VMEM)


def lanes_of(q):
    return slice(q * LANES, (q + 1) * LANES)


def rows_of(t):
    return pl.ds(pl.multiple_of(t * 8, 8), 8)


def solve_tile(t, row_of, inv_ref, live):
    keep = (lax.broadcasted_iota(jnp.int32, (8, LANES), 0) < NVAR) & live
    blocks = []
    for q in range(inv_ref.shape[3] // LANES):
        total = None
        for j in range(inv_ref.shape[1]):
            term = inv_ref[t, j, :, lanes_of(q)].astype(F32) * row_of(q, j)
            total = term if total is None else total + term
        blocks.append(jnp.where(keep, total, 0.0))
    return blocks


def pack_sent(adj_ref, send_ref, sent_ref):
    for s in range(send_ref.shape[1]):
        here = rows_of(send_ref[0, s])
        for q in range(adj_ref.shape[0]):
            sent_ref[q, NVAR * s : NVAR * (s + 1), :] = adj_ref[q, here, :][:NVAR]


def fetch(pairs, sems):
    copies = [pltpu.make_async_copy(src, dst, sems.at[i]) for i, (src, dst) in enumerate(pairs)]
    for copy in copies:
        copy.start()
    return copies


def put_rows(adj_ref, t, blocks):
    for q, block in enumerate(blocks):
        adj_ref[q, rows_of(t), :] = block


def first_kernel(
    send_hbm, near_hbm, count_ref, rhs_hbm, inv_hbm,
    adj_ref, sent_ref, rhs_ref, inv_ref, send_ref, near_ref, listed_ref, sems, table_sems,
):
    send_copy, near_copy = fetch(((send_hbm, send_ref), (near_hbm, near_ref)), table_sems)
    tiles, sends = rhs_ref.shape[0], send_ref.shape[1]
    half = tiles // 2
    pairs = [(rhs_hbm, rhs_ref)]
    pairs += [(inv_hbm.at[pl.ds(p * half, half)], inv_ref.at[pl.ds(p * half, half)]) for p in range(2)]
    copies = fetch(pairs, sems)
    send_copy.wait()
    for t in range(tiles):
        listed_ref[0, t] = 0
    for s in range(sends):
        listed_ref[0, send_ref[0, s]] = 1
    for copy in copies:
        copy.wait()

    @pl.loop(0, sends)
    def _(s):
        t = send_ref[0, s]
        row_of = lambda q, j: rhs_ref[t, j : j + 1, lanes_of(q)]
        put_rows(adj_ref, t, solve_tile(t, row_of, inv_ref, t < count_ref[0]))

    pack_sent(adj_ref, send_ref, sent_ref)
    near_copy.wait()


def first_rest_kernel(listed_ref, count_ref, rhs_ref, inv_ref, lead_ref, cpl_hbm, adj_ref, cpl_ref, sems):
    parts = sems.shape[0]
    step = cpl_ref.shape[0] // parts
    some = [pl.ds(p * step, step) for p in range(parts)]
    copies = fetch([(cpl_hbm.at[s], cpl_ref.at[s]) for s in some], sems)
    adj_ref[...] = lead_ref[...]

    @pl.loop(0, rhs_ref.shape[0])
    def _(t):
        @pl.when(listed_ref[0, t] == 0)
        def _():
            row_of = lambda q, j: rhs_ref[t, j : j + 1, lanes_of(q)]
            put_rows(adj_ref, t, solve_tile(t, row_of, inv_ref, t < count_ref[0]))

    for copy in copies:
        copy.wait()


def halo_place(name):
    odd_region = lax.axis_index("region") % 2
    odd_sub = lax.axis_index("sub") % 2
    return {"ra": 1 - odd_region, "rb": odd_region, "sa": 3 - odd_sub, "sb": 2 + odd_sub}[name]


def build_extended(order, old_ref, halo_refs, ext_ref):
    own = old_ref.shape[1]
    ext_ref[:, :own, :] = old_ref[...]
    for name, halo in zip(order, halo_refs):
        width = halo.shape[1]
        ext_ref[:, pl.ds(pl.multiple_of(own + halo_place(name) * width, 8), width), :] = halo[...]


def sweep_tile(t, near_ref, count_ref, rhs_ref, inv_ref, cpl_ref, ext_ref, resid_ref):
    own = rhs_ref.shape[0]
    bases = []
    for k in range(cpl_ref.shape[1]):
        tile = near_ref[k, t]
        bases.append(jnp.where(tile < own, tile * 8, tile * NVAR + own * (8 - NVAR)))
    for q in range(resid_ref.shape[0]):
        sums = [rhs_ref[t, :, lanes_of(q)], None]
        for k, base in enumerate(bases):
            for m in range(NVAR):
                term = cpl_ref[t, k, m, :, lanes_of(q)].astype(F32) * ext_ref[q, pl.ds(base + m, 1), :]
                if k % 2:
                    sums[1] = term if sums[1] is None else sums[1] + term
                else:
                    sums[0] = sums[0] - term
        resid_ref[q] = sums[0] - sums[1]
    return solve_tile(t, lambda q, j: resid_ref[q, j : j + 1, :], inv_ref, t < count_ref[0])


def lead_kernel(
    order, near_ref, send_ref, count_ref, rhs_ref, inv_ref, cpl_ref, old_ref, h0, h1, h2, h3,
    adj_ref, sent_ref, ext_ref, resid_ref,
):
    build_extended(order, old_ref, (h0, h1, h2, h3), ext_ref)

    @pl.loop(0, send_ref.shape[1])
    def _(s):
        t = send_ref[0, s]
        put_rows(adj_ref, t, sweep_tile(t, near_ref, count_ref, rhs_ref, inv_ref, cpl_ref, ext_ref, resid_ref))

    pack_sent(adj_ref, send_ref, sent_ref)


def rest_kernel(
    near_ref, listed_ref, count_ref, rhs_ref, inv_ref, cpl_ref, ext_ref, lead_ref, adj_ref, resid_ref
):
    adj_ref[...] = lead_ref[...]

    @pl.loop(0, rhs_ref.shape[0])
    def _(t):
        @pl.when(listed_ref[0, t] == 0)
        def _():
            put_rows(adj_ref, t, sweep_tile(t, near_ref, count_ref, rhs_ref, inv_ref, cpl_ref, ext_ref, resid_ref))


def early_kernel(
    order, near_ref, count_ref, rhs_ref, inv_ref, cpl_ref, old_ref, h0, h1, h2, adj_ref, ext_ref, late_ref, resid_ref
):
    build_extended(order, old_ref, (h0, h1, h2), ext_ref)
    tiles, group = rhs_ref.shape[0], h0.shape[1] // NVAR
    first = tiles + halo_place("sb") * group

    @pl.loop(0, tiles)
    def _(t):
        late = jnp.int32(0)
        for k in range(cpl_ref.shape[1]):
            tile = near_ref[k, t]
            late = late + jnp.where((tile >= first) & (tile < first + group), 1, 0)
        late_ref[0, t] = late

        @pl.when(late == 0)
        def _():
            put_rows(adj_ref, t, sweep_tile(t, near_ref, count_ref, rhs_ref, inv_ref, cpl_ref, ext_ref, resid_ref))


def last_kernel(
    near_ref, count_ref, late_ref, rhs_ref, inv_ref, cpl_ref, hess_ref, early_ref, old_ext_ref, halo_ref,
    vertex_ref, region_ref, slot_ref, rank_hot_ref,
    adj_hbm, metric_hbm, parcel_ref,
    ext_ref, resid_ref, adj_ref, metric_ref, column_ref, gathered_ref, out_sems,
):
    ext_ref[...] = old_ext_ref[...]
    own, group = rhs_ref.shape[0] * 8, halo_ref.shape[1]
    ext_ref[:, pl.ds(pl.multiple_of(own + halo_place("sb") * group, 8), group), :] = halo_ref[...]
    tiles, width = rhs_ref.shape[0], rhs_ref.shape[2]
    chunks = width // LANES

    def put(t, blocks):
        for q, block in enumerate(blocks):
            adj_ref[rows_of(t), lanes_of(q)] = block
            column_ref[q, rows_of(t), :] = jnp.abs(block)

    @pl.loop(0, tiles)
    def _(t):
        @pl.when(late_ref[0, t] == 0)
        def _():
            put(t, [early_ref[q, rows_of(t), :] for q in range(chunks)])

        @pl.when(late_ref[0, t] != 0)
        def _():
            put(t, sweep_tile(t, near_ref, count_ref, rhs_ref, inv_ref, cpl_ref, ext_ref, resid_ref))

    adj_out = pltpu.make_async_copy(adj_ref, adj_hbm, out_sems.at[0])
    adj_out.start()

    for q in range(chunks):
        sums = [None] * 6
        for c in range(NVAR):
            size = column_ref[q, pl.ds(c, tiles, stride=8), :]
            for s in range(6):
                term = hess_ref[c, s, :, lanes_of(q)].astype(F32) * size
                sums[s] = term if sums[s] is None else sums[s] + term
        for s in range(6):
            metric_ref[s, :, lanes_of(q)] = sums[s]
    metric_out = pltpu.make_async_copy(metric_ref, metric_hbm, out_sems.at[1])
    metric_out.start()

    entries = vertex_ref.shape[1]
    in_tile = lax.broadcasted_iota(jnp.int32, (8, LANES), 0)

    for g in range(entries // LANES):
        here = lanes_of(g)
        vertex = vertex_ref[:, here]
        row = jnp.broadcast_to(vertex // LANES, (8, LANES))
        lane = jnp.broadcast_to(vertex % LANES, (8, LANES))
        sums = [jnp.zeros((8, LANES), F32)] * 6
        for q in range(chunks):
            for h in range(tiles // 8):
                mine = row == (in_tile + h * 8) * chunks + q
                for s in range(6):
                    block = metric_ref[s, h * 8 : (h + 1) * 8, q * LANES : (q + 1) * LANES]
                    sums[s] = jnp.where(mine, jnp.take_along_axis(block, lane, axis=1), sums[s])
        for s in range(6):
            gathered_ref[s : s + 1, here] = jnp.sum(sums[s], axis=0, keepdims=True)

    values = gathered_ref[...]
    which = lax.broadcasted_iota(jnp.int32, values.shape, 0)
    values = jnp.where(which == NVAR, slot_ref[...].astype(F32), jnp.where(which < NVAR, values, 0.0))
    high = values.astype(BF16).astype(F32)
    low = values - high

    regions = parcel_ref.shape[0]
    dest = region_ref[...]
    half = regions // 2

    for part in range(2):
        pieces = []
        for piece in (high, low):
            for d in range(half):
                pieces.append(jnp.where(dest == part * half + d, piece, 0.0))
        left = jnp.concatenate(pieces, axis=0).astype(BF16)
        placed = lax.dot_general(left, rank_hot_ref[...], (((1,), (1,)), ((), ())), preferred_element_type=F32)
        placed = placed[: half * 8] + placed[half * 8 :]
        for d in range(half):
            parcel_ref[part * half + d] = placed[d * 8 : (d + 1) * 8]
    adj_out.wait()
    metric_out.wait()


def rank_kernel(region_ref, hot_ref, rank_ref):
    entries = region_ref.shape[1]
    regions = 32
    upper = (
        lax.broadcasted_iota(jnp.int32, (LANES, LANES), 0) <= lax.broadcasted_iota(jnp.int32, (LANES, LANES), 1)
    )
    upper = jnp.where(upper, 1.0, 0.0).astype(BF16)
    region_id = lax.broadcasted_iota(jnp.int32, (regions, LANES), 0)
    carry = jnp.zeros((regions, 1), F32)
    for g in range(entries // LANES):
        here = region_id == region_ref[:, g * LANES : (g + 1) * LANES]
        hot = jnp.where(here, 1.0, 0.0)
        count = lax.dot_general(hot.astype(BF16), upper, (((1,), (0,)), ((), ())), preferred_element_type=F32) + carry
        rank_ref[:, g * LANES : (g + 1) * LANES] = jnp.sum(
            jnp.where(here, count - 1.0, 0.0), axis=0, keepdims=True
        )
        carry = count[:, LANES - 1 :]
    rank = rank_ref[...].astype(jnp.int32)
    places = lax.broadcasted_iota(jnp.int32, (CAP, entries), 0)
    hot_ref[...] = jnp.where(places == rank, 1.0, 0.0).astype(BF16)


def owner_kernel(parcel_ref, owned_ref):
    regions = parcel_ref.shape[0]
    highs = OWNED // LANES
    row_high = lax.broadcasted_iota(jnp.int32, (highs * 8, LANES), 0) // 8
    low_id = lax.broadcasted_iota(jnp.int32, (LANES, LANES), 0)
    total = jnp.zeros((2 * highs * 8, LANES), F32)
    for r in range(0, regions, 2):
        lefts, rights = [], []
        for q in (r, r + 1):
            block = parcel_ref[q]
            slot = block[NVAR : NVAR + 1, :].astype(jnp.int32)
            high = block.astype(BF16).astype(F32)
            low = block - high
            mask = row_high == slot // LANES
            tall_h = jnp.where(mask, jnp.concatenate([high] * highs, axis=0), 0.0)
            tall_l = jnp.where(mask, jnp.concatenate([low] * highs, axis=0), 0.0)
            lefts.append(jnp.concatenate([tall_h, tall_l], axis=0).astype(BF16))
            rights.append(jnp.where(low_id == slot % LANES, 1.0, 0.0).astype(BF16))
        left = jnp.concatenate(lefts, axis=1)
        right = jnp.concatenate(rights, axis=1)
        total += lax.dot_general(left, right, (((1,), (1,)), ((), ())), preferred_element_type=F32)
    total = total[: highs * 8] + total[highs * 8 :]
    for h in range(highs):
        owned_ref[:, h * LANES : (h + 1) * LANES] = total[h * 8 : h * 8 + NVAR]


def pairings():
    def swap(axis, first):
        length = lax.axis_size(axis)
        return axis, [p for i in range(first, length - 1, 2) for p in ((i, i + 1), (i + 1, i))]

    return {"ra": swap("region", 0), "rb": swap("region", 1), "sa": swap("sub", 0), "sb": swap("sub", 1)}


def exchange(sent, order):
    pairs = pairings()
    return [lax.ppermute(sent, *pairs[name]) for name in order]


def per_device(
    rhs, diag_inv, coupling, neighbours, send_tiles, tile_count, hessian, shared_vertex, owner_region, owner_slot
):
    tiles, block, width = rhs.shape
    sends = send_tiles.shape[1]
    entries = shared_vertex.shape[0]
    regions = lax.axis_size("region")
    params = pltpu.CompilerParams(vmem_limit_bytes=40 * 2**20)
    rhs = pltpu.with_memory_space_constraint(rhs, pltpu.HBM)
    diag_inv = pltpu.with_memory_space_constraint(diag_inv, pltpu.HBM)
    coupling = pltpu.with_memory_space_constraint(coupling, pltpu.HBM)
    neighbours = pltpu.with_memory_space_constraint(neighbours.T, pltpu.HBM)
    send_tiles = pltpu.with_memory_space_constraint(send_tiles, pltpu.HBM)
    vertex = shared_vertex.reshape(1, entries)
    dest = owner_region.reshape(1, entries)
    slot = owner_slot.reshape(1, entries)

    chunks = width // LANES
    adj_shape = jax.ShapeDtypeStruct((chunks, tiles * 8, LANES), F32)
    sent_shape = jax.ShapeDtypeStruct((chunks, sends * NVAR, LANES), F32)
    ext_shape = jax.ShapeDtypeStruct((chunks, tiles * 8 + 4 * sends * NVAR, LANES), F32)
    resid = pltpu.VMEM((chunks, 8, LANES), F32)
    hbm = pl.BlockSpec(memory_space=pltpu.HBM)
    smem = pl.BlockSpec(memory_space=pltpu.SMEM)
    scalars = functools.partial(pltpu.with_memory_space_constraint, memory_space=pltpu.SMEM)
    beside = pl.CostEstimate(flops=0, bytes_accessed=4 * 2**20, transcendentals=0)

    lead, sent, rhs, diag_inv, send_tiles, neighbours, listed = pl.pallas_call(
        first_kernel,
        out_shape=(
            adj_shape,
            sent_shape,
            jax.ShapeDtypeStruct(rhs.shape, rhs.dtype),
            jax.ShapeDtypeStruct(diag_inv.shape, diag_inv.dtype),
            pltpu.SMEM(send_tiles.shape, jnp.int32),
            pltpu.SMEM(neighbours.shape, jnp.int32),
            pltpu.SMEM((1, tiles), jnp.int32),
        ),
        in_specs=[hbm, hbm, smem, hbm, hbm],
        out_specs=(VMEM,) * 4 + (smem,) * 3,
        scratch_shapes=[pltpu.SemaphoreType.DMA((3,)), pltpu.SemaphoreType.DMA((2,))],
        compiler_params=params,
        name="first",
    )(send_tiles, neighbours, tile_count, rhs, diag_inv)
    send_tiles, neighbours, listed = scalars(send_tiles), scalars(neighbours), scalars(listed)
    halos = exchange(sent, ORDER)
    adjoint, coupling = pl.pallas_call(
        first_rest_kernel,
        out_shape=(adj_shape, jax.ShapeDtypeStruct(coupling.shape, coupling.dtype)),
        in_specs=[smem, smem, VMEM, VMEM, VMEM, hbm],
        out_specs=(VMEM, VMEM),
        scratch_shapes=[pltpu.SemaphoreType.DMA((tiles,))],
        compiler_params=params,
        cost_estimate=pl.CostEstimate(flops=0, bytes_accessed=4 * coupling.size, transcendentals=0),
        name="first_rest",
    )(listed, tile_count, rhs, diag_inv, lead, coupling)
    rank_hot = pl.pallas_call(
        rank_kernel,
        out_shape=jax.ShapeDtypeStruct((CAP, entries), BF16),
        in_specs=[VMEM],
        out_specs=VMEM,
        scratch_shapes=[pltpu.VMEM((1, entries), F32)],
        compiler_params=params,
        name="rank",
    )(dest)
    for sweep in range(SWEEPS - 1):
        order = LAST_ORDER if sweep == SWEEPS - 2 else ORDER
        lead, sent, extended = pl.pallas_call(
            functools.partial(lead_kernel, ORDER),
            out_shape=(adj_shape, sent_shape, ext_shape),
            in_specs=[smem] * 3 + [VMEM] * 8,
            out_specs=(VMEM,) * 3,
            scratch_shapes=[resid],
            compiler_params=params,
            name="lead",
        )(neighbours, send_tiles, tile_count, rhs, diag_inv, coupling, adjoint, *halos)
        halos = exchange(sent, order)
        adjoint = pl.pallas_call(
            rest_kernel,
            out_shape=adj_shape,
            in_specs=[smem] * 3 + [VMEM] * 5,
            out_specs=VMEM,
            scratch_shapes=[resid],
            compiler_params=params,
            cost_estimate=beside,
            name="rest",
        )(neighbours, listed, tile_count, rhs, diag_inv, coupling, extended, lead)
    by_name = dict(zip(LAST_ORDER, halos))
    here = tuple(name for name in LAST_ORDER if name != "sb")
    early, extended, late = pl.pallas_call(
        functools.partial(early_kernel, here),
        out_shape=(adj_shape, ext_shape, pltpu.SMEM((1, tiles), jnp.int32)),
        in_specs=[smem] * 2 + [VMEM] * 7,
        out_specs=(VMEM, VMEM, smem),
        scratch_shapes=[resid],
        compiler_params=params,
        cost_estimate=beside,
        name="early",
    )(neighbours, tile_count, rhs, diag_inv, coupling, adjoint, *(by_name[name] for name in here))
    out, metric, parcels = pl.pallas_call(
        last_kernel,
        out_shape=(
            jax.ShapeDtypeStruct((tiles * 8, width), F32),
            jax.ShapeDtypeStruct((6, tiles, width), F32),
            jax.ShapeDtypeStruct((regions, 8, CAP), F32),
        ),
        in_specs=[smem] * 3 + [VMEM] * 11,
        out_specs=(hbm, hbm, VMEM),
        scratch_shapes=[
            pltpu.VMEM(ext_shape.shape, F32),
            resid,
            pltpu.VMEM((tiles * 8, width), F32),
            pltpu.VMEM((6, tiles, width), F32),
            pltpu.VMEM((chunks, tiles * 8, LANES), F32),
            pltpu.VMEM((8, entries), F32),
            pltpu.SemaphoreType.DMA((2,)),
        ],
        compiler_params=params,
        name="last",
    )(
        neighbours, tile_count, scalars(late), rhs, diag_inv, coupling, hessian.transpose(1, 2, 0, 3), early, extended,
        by_name["sb"],
        vertex, dest, slot, rank_hot,
    )
    out = out.reshape(tiles, block, width)
    metric = metric.transpose(1, 0, 2)
    parcels = lax.all_to_all(parcels, "region", 0, 0, tiled=True)
    owned = pl.pallas_call(
        owner_kernel,
        out_shape=jax.ShapeDtypeStruct((6, OWNED), F32),
        in_specs=[VMEM],
        out_specs=VMEM,
        compiler_params=params,
        name="owner",
    )(parcels)
    return out, metric, owned


def solution(mesh):
    both = ("region", "sub")
    placed = (
        P(both, None, None),
        P(both, None, None, None),
        P(both, None, None, None, None),
        P(both, None),
        P(both, None),
        P(both),
        P(both, None, None, None),
        P(both),
        P(both, None),
        P(both),
    )
    return jax.shard_map(
        per_device,
        mesh=mesh,
        in_specs=placed,
        out_specs=(P(both, None, None), P(both, None, None), P(None, both)),
        check_vma=False,
    )
```
